32 devices in a mesh: dp: 8 (over z, y), tensor: 4 (over x, core).
Axes of the slice: x: 2, y: 2, z: 4, core: 2. Of those that a mesh axis runs over, the one named last changes fastest.
Arguments:
- tokens: bfloat16 [24, 1024, 1536], P('dp'), may hold values from -6 to 6
- cotangent: bfloat16 [24, 1024, 1536], P('dp'), may hold values from -6 to 6
- norm_gain: float32 [1536], replicated, may hold values from 0.8 to 6, as said below
- w_zx: float32 [1536, 2, 3072], P('dp', None, 'tensor'), may hold values from -0.15625 to 0.15625
- state_proj_weight: float32 [1536, 256], P('dp'), may hold values from -0.15625 to 0.15625
- step_weight: float32 [1536, 48], P('dp', 'tensor'), may hold values from -0.078125 to 0.078125
- exit_coefficient_matrix: float32 [3072, 1536], P('tensor', 'dp'), may hold values from -0.0546875 to 0.0546875
- x_params: float32 [6, 3072], P(None, 'tensor')
- bc_params: float32 [5, 256], replicated
- head_params: float32 [3, 48], P(None, 'tensor'), may hold values from -9.3 to 2.8, as said below
- zx_moment: float32 [1536, 2, 3072], P('dp', None, 'tensor'), may hold values from -448 to 448
- bc_moment: float32 [1536, 256], P('dp'), may hold values from -448 to 448
- dt_moment: float32 [1536, 48], P('dp', 'tensor'), may hold values from -112 to 112
- out_moment: float32 [3072, 1536], P('tensor', 'dp'), may hold values from -448 to 448
- gain_moment: float32 [1536], replicated, may hold values from -448 to 448
- xpar_moment: float32 [6, 3072], P(None, 'tensor'), may hold values from -448 to 448
- bcpar_moment: float32 [5, 256], replicated, may hold values from -448 to 448
- head_moment: float32 [3, 48], P(None, 'tensor'), may hold values from -448 to 448
Outputs:
- result: bfloat16 [24, 1024, 1536], P('dp', None, 'tensor')
- input_grad: float32 [24, 1024, 1536], P('dp', None, 'tensor')
- zx_moment_new: float32 [1536, 2, 3072], P('dp', None, 'tensor')
- zx_new: float32 [1536, 2, 3072], P('dp', None, 'tensor')
- bc_moment_new: float32 [1536, 256], P('dp')
- bc_new: float32 [1536, 256], P('dp')
- dt_moment_new: float32 [1536, 48], P('dp', 'tensor')
- dt_new: float32 [1536, 48], P('dp', 'tensor')
- out_moment_new: float32 [3072, 1536], P('tensor', 'dp')
- out_new: float32 [3072, 1536], P('tensor', 'dp')
- gain_moment_new: float32 [1536], replicated
- gain_new: float32 [1536], replicated
- xpar_moment_new: float32 [6, 3072], P(None, 'tensor')
- xpar_new: float32 [6, 3072], P(None, 'tensor')
- bcpar_moment_new: float32 [5, 256], replicated
- bcpar_new: float32 [5, 256], replicated
- head_moment_new: float32 [3, 48], P(None, 'tensor')
- head_new: float32 [3, 48], P(None, 'tensor')
The draws below stay inside these ranges and needn't reach their ends.
Inputs may be any that keep to these rules, and one draw needn't show every extreme that they name: `norm_gain`: positive, varying along the features. `head_params`: row 0 is the log of a positive decay rate, row 1 a step bias, row 2 a positive skip gain.
All inputs are finite; a program needn't handle non-finite values.
Results may differ from the reference program's by a relative error of at most 0.012.
The reference program's roundings to bfloat16 on the way count: a program that leaves them out, or rounds other values in their place, can miss the bound.
Values may be sent and summed in bfloat16 or wider, within the bound.
No kernel may reach another device: no remote copies, remote signals or barrier semaphores. Data moves between devices by JAX's collectives and lax.ppermute only.
A program may use at most 320 MiB of HBM per device.

```python
import jax
import jax.numpy as jnp
from jax import lax

D = 1536
H = 48
P_SIZE = 64
NS = 128
KW = 4
GROUP = 256
LEN = 1024
SEQS = 24
INNER = 3072


def ramp_scale(entries, ramp_top):
    return 1.0 + (ramp_top - 1.0) * jnp.arange(entries, dtype=jnp.float32) / (entries - 1)


def draw_norm_gain(key, part):
    key = jax.random.fold_in(key, 11)
    ramp_top = 3.0
    jitter = jax.random.uniform(key, (D,), jnp.float32, 0.8, 1.2)
    return ramp_scale(D, ramp_top) * jitter


def draw_x_params(key, part):
    key = jax.random.fold_in(key, 12)
    subkeys = jax.random.split(key, 3)
    ramp_top = 3.0
    ramp = ramp_scale(INNER, ramp_top)
    conv_taps = jax.random.normal(subkeys[0], (KW, INNER), jnp.float32) * 0.35 * jnp.sqrt(ramp)
    conv_bias = jax.random.normal(subkeys[1], (1, INNER), jnp.float32) * 0.3
    gate_gain = ramp[None] * jax.random.uniform(subkeys[2], (1, INNER), jnp.float32, 0.8, 1.2)
    return jnp.concatenate([conv_taps, conv_bias, gate_gain], axis=0)


def draw_bc_params(key, part):
    key = jax.random.fold_in(key, 13)
    subkeys = jax.random.split(key, 2)
    conv_taps = jax.random.normal(subkeys[0], (KW, 2 * NS), jnp.float32) * 0.35
    conv_bias = jax.random.normal(subkeys[1], (1, 2 * NS), jnp.float32) * 0.3
    return jnp.concatenate([conv_taps, conv_bias], axis=0)


def draw_head_params(key, part):
    key = jax.random.fold_in(key, 14)
    subkeys = jax.random.split(key, 3)
    rate_top = 16.0
    step_low = -6.9
    step_high = -2.3
    log_rate = jax.random.uniform(subkeys[0], (1, H), jnp.float32, 0.0, jnp.log(rate_top))
    step_init = jnp.exp(jax.random.uniform(subkeys[1], (1, H), jnp.float32, step_low, step_high))
    step_bias = jnp.log(jnp.expm1(step_init))
    skip_gain = jax.random.uniform(subkeys[2], (1, H), jnp.float32, 0.5, 1.5)
    return jnp.concatenate([log_rate, step_bias, skip_gain], axis=0)


def shard_levels(rng, dims, shards, low, largest):
    level = 1.0
    for dim, shards_of in shards:
        draws = jax.random.uniform(jax.random.fold_in(jax.random.fold_in(rng, 6), dim), (shards_of,), jnp.float32, low / len(shards), largest / len(shards))
        level = level * jnp.repeat(jnp.exp(draws), dims[dim] // shards_of).reshape((-1,) + (1,) * (len(dims) - 1 - dim))
    return level


def normal_values(stream_key, dims, spread, limit, cuts=(), held_as=jnp.bfloat16):
    values = jax.random.normal(stream_key, dims, jnp.float32) * spread
    if len(cuts) > 0:
        values = shard_levels(stream_key, dims, cuts, -0.22, 0.18) * values
    return jnp.clip(values, min=-limit, max=limit).astype(held_as)


def setup_inputs(seed: int = 0) -> dict:
    arg_keys = jax.random.split(jax.random.key(seed), 19)
    tokens = normal_values(arg_keys[0], (SEQS, LEN, D), 1.0, 6.0, ((0, 8),))
    cotangent = normal_values(arg_keys[1], (SEQS, LEN, D), 1.0, 6.0, ((0, 8),))
    norm_gain = draw_norm_gain(jax.random.fold_in(arg_keys[18], 71), 0)
    w_zx = normal_values(arg_keys[3], (D, 2, INNER), D ** -0.5, 0.15625, ((0, 8), (2, 4)), jnp.float32)
    state_proj_weight = normal_values(arg_keys[4], (D, 2 * NS), D ** -0.5, 0.15625, ((0, 8),), jnp.float32)
    step_weight = normal_values(arg_keys[5], (D, H), (4 * D) ** -0.5, 0.078125, ((0, 8), (1, 4)), jnp.float32)
    exit_coefficient_matrix = normal_values(arg_keys[6], (INNER, D), (4 * INNER) ** -0.5, 0.0546875, ((0, 4), (1, 8)), jnp.float32)
    x_params = draw_x_params(jax.random.fold_in(arg_keys[18], 71), 0)
    bc_params = draw_bc_params(jax.random.fold_in(arg_keys[18], 71), 0)
    head_params = draw_head_params(jax.random.fold_in(arg_keys[18], 71), 0)
    zx_moment = normal_values(arg_keys[10], (D, 2, INNER), ((SEQS * LEN) ** 0.5 / 2), 448.0, ((0, 8), (2, 4)), jnp.float32)
    bc_moment = normal_values(arg_keys[11], (D, 2 * NS), ((SEQS * LEN) ** 0.5 / 2), 448.0, ((0, 8),), jnp.float32)
    dt_moment = normal_values(arg_keys[12], (D, H), ((SEQS * LEN) ** 0.5 / 8), 112.0, ((0, 8), (1, 4)), jnp.float32)
    out_moment = normal_values(arg_keys[13], (INNER, D), ((SEQS * LEN) ** 0.5 / 2), 448.0, ((0, 4), (1, 8)), jnp.float32)
    gain_moment = normal_values(arg_keys[14], (D,), ((SEQS * LEN) ** 0.5 / 2), 448.0, (), jnp.float32)
    xpar_moment = normal_values(arg_keys[15], (KW + 2, INNER), ((SEQS * LEN) ** 0.5 / 2), 448.0, ((1, 4),), jnp.float32)
    bcpar_moment = normal_values(arg_keys[16], (KW + 1, 2 * NS), ((SEQS * LEN) ** 0.5 / 2), 448.0, (), jnp.float32)
    head_moment = normal_values(arg_keys[17], (3, H), ((SEQS * LEN) ** 0.5 / 2), 448.0, ((1, 4),), jnp.float32)
    return dict(tokens=tokens, cotangent=cotangent, norm_gain=norm_gain, w_zx=w_zx, state_proj_weight=state_proj_weight, step_weight=step_weight, exit_coefficient_matrix=exit_coefficient_matrix, x_params=x_params, bc_params=bc_params, head_params=head_params, zx_moment=zx_moment, bc_moment=bc_moment, dt_moment=dt_moment, out_moment=out_moment, gain_moment=gain_moment, xpar_moment=xpar_moment, bcpar_moment=bcpar_moment, head_moment=head_moment)


@jax.custom_vjp
def coarse_arithmetic_mode(v):
    return lax.optimization_barrier(v.astype(jnp.bfloat16)).astype(jnp.float32)

@jax.custom_vjp
def lower_precision_backward(v):
    return v

def low_keep(v):
    return (coarse_arithmetic_mode(v), None)

def low_pass(kept, grad):
    return (grad,)

def back_keep(v):
    return (v, None)

def back_low(kept, grad):
    return (coarse_arithmetic_mode(grad),)
coarse_arithmetic_mode.defvjp(low_keep, low_pass)
lower_precision_backward.defvjp(back_keep, back_low)
finest_arithmetic_mode = lax.Precision.HIGHEST
norm_eps = 1e-05
poly_first = 3.4445
poly_second = -4.775
poly_third = 2.0315
momentum_rate = 0.95
matrix_rate = 0.5
weight_decay = 0.1
small_rate = 0.0025

def conv_silu(signal, conv_taps, conv_bias):
    width_taps = conv_taps.shape[0]
    length = signal.shape[1]
    padded = jnp.pad(signal, ((0, 0), (width_taps - 1, 0), (0, 0)))
    summed = conv_bias + sum((conv_taps[offset] * padded[:, offset:offset + length] for offset in range(width_taps)))
    return jax.nn.silu(summed)

def block_step(state_carry, pieces, skip_gain):
    block_x, block_b, block_c, block_decay, block_size = pieces
    span = block_x.shape[1]
    running = jnp.cumsum(block_decay, axis=1)
    by_head = jnp.swapaxes(running, 1, 2)
    log_gap = by_head[:, :, :, None] - by_head[:, :, None, :]
    later = lax.broadcasted_iota(jnp.int32, (span, span), 0)
    earlier = lax.broadcasted_iota(jnp.int32, (span, span), 1)
    causal = later >= earlier
    kernel = jnp.where(causal, jnp.exp(jnp.where(causal, log_gap, 0.0)), 0.0)
    scores = jnp.einsum('stn,sun->stu', block_c, block_b, precision=finest_arithmetic_mode)
    weighted = kernel * scores[:, None]
    scaled_x = block_x * block_size[..., None]
    inside = jnp.einsum('shtu,suhp->sthp', weighted, scaled_x, precision=finest_arithmetic_mode)
    carried = jnp.einsum('stn,shpn->sthp', block_c, state_carry, precision=finest_arithmetic_mode) * jnp.exp(running)[..., None]
    tail_decay = jnp.exp(running[:, -1:, :] - running)
    renewed = state_carry * jnp.exp(running[:, -1, :])[:, :, None, None] + jnp.einsum('suhp,sun->shpn', scaled_x * tail_decay[..., None], block_b, precision=finest_arithmetic_mode)
    return (renewed, inside + carried + skip_gain[:, None] * block_x)

def mixer(conv_x, conv_bc, step_preactivation, head_params):
    sequences, length, inner_width = conv_x.shape
    head_count = head_params.shape[1]
    head_width = inner_width // head_count
    state_width = conv_bc.shape[2] // 2
    blocks = length // GROUP
    step_size = jax.nn.softplus(step_preactivation + head_params[1])
    log_decay = -step_size * jnp.exp(head_params[0])

    def to_blocks(array):
        shaped = array.reshape((sequences, blocks, length // blocks) + array.shape[2:])
        return jnp.moveaxis(shaped, 1, 0)
    pieces = (to_blocks(conv_x.reshape(sequences, length, head_count, head_width)), to_blocks(conv_bc[:, :, :state_width]), to_blocks(conv_bc[:, :, state_width:]), to_blocks(log_decay), to_blocks(step_size))
    start_state = jnp.zeros((sequences, head_count, head_width, state_width), jnp.float32)
    stepper = jax.checkpoint(lambda state_carry, block_pieces: block_step(state_carry, block_pieces, head_params[2]))
    final_state, outputs = lax.scan(stepper, start_state, pieces)
    return jnp.moveaxis(outputs, 0, 1).reshape(sequences, length, inner_width)

def forward(entering_token_vectors, norm_gain, w_zx, state_proj_weight, step_weight, exit_coefficient_matrix, x_params, bc_params, head_params):
    kwidth = bc_params.shape[0] - 1
    inv_rms = lax.rsqrt(lax.optimization_barrier(jnp.mean(entering_token_vectors * entering_token_vectors, axis=-1, keepdims=True)) + norm_eps)
    normalized_input = coarse_arithmetic_mode(entering_token_vectors * inv_rms * norm_gain)
    gate_input_lower = coarse_arithmetic_mode(w_zx)
    gate_preactivation = lower_precision_backward(jnp.einsum('gtc,cu->gtu', normalized_input, gate_input_lower[:, 0], precision=finest_arithmetic_mode))
    convolve_input = lower_precision_backward(jnp.einsum('gtc,cu->gtu', normalized_input, gate_input_lower[:, 1], precision=finest_arithmetic_mode))
    state_proj_preconv = lower_precision_backward(jnp.einsum('gmq,qp->gmp', normalized_input, coarse_arithmetic_mode(state_proj_weight), precision=finest_arithmetic_mode))
    step_preactivation = lower_precision_backward(jnp.einsum('bpj,jt->bpt', normalized_input, coarse_arithmetic_mode(step_weight), precision=finest_arithmetic_mode))
    conv_x = coarse_arithmetic_mode(conv_silu(convolve_input, x_params[:kwidth], x_params[kwidth]))
    conv_bc = coarse_arithmetic_mode(conv_silu(state_proj_preconv, bc_params[:kwidth], bc_params[kwidth]))
    mixed_y = mixer(conv_x, conv_bc, step_preactivation, head_params)
    gated = mixed_y * jax.nn.silu(gate_preactivation)
    inverse = lax.rsqrt(lax.optimization_barrier(jnp.mean(gated * gated, axis=-1, keepdims=True)) + norm_eps)
    blended_result_vectors = coarse_arithmetic_mode(gated * inverse * x_params[kwidth + 1])
    return entering_token_vectors + jnp.einsum('gkt,to->gko', blended_result_vectors, coarse_arithmetic_mode(exit_coefficient_matrix), precision=finest_arithmetic_mode)

def to_matrices(zx_in, bc_in, dt_in, out_in, head_width):
    row_count = zx_in.shape[0]
    head_count = dt_in.shape[1]
    state_width = bc_in.shape[1] // 2
    zx_mats = jnp.transpose(zx_in.reshape(row_count, 2, head_count, head_width), (1, 2, 0, 3)).reshape(2 * head_count, row_count, head_width)
    out_mats = jnp.transpose(out_in.reshape(head_count, head_width, row_count), (0, 2, 1))
    head_mats = jnp.concatenate([zx_mats, out_mats], axis=0)
    bc_mats = jnp.transpose(bc_in.reshape(row_count, 2, state_width), (1, 0, 2))
    dt_mats = jnp.transpose(dt_in, (1, 0))[:, :, None]
    return (head_mats, bc_mats, dt_mats)

def from_matrices(head_mats, bc_mats, dt_mats):
    head_count = dt_mats.shape[0]
    row_count = head_mats.shape[1]
    head_width = head_mats.shape[2]
    zx_mats = head_mats[:2 * head_count].reshape(2, head_count, row_count, head_width)
    zx_back = jnp.transpose(zx_mats, (2, 0, 1, 3)).reshape(row_count, 2, head_count * head_width)
    out_back = jnp.transpose(head_mats[2 * head_count:], (0, 2, 1)).reshape(head_count * head_width, row_count)
    bc_back = jnp.transpose(bc_mats, (1, 0, 2)).reshape(row_count, -1)
    dt_back = jnp.transpose(dt_mats[:, :, 0], (1, 0))
    return (zx_back, bc_back, dt_back, out_back)

def gram_of(square_array_operand):
    return jnp.einsum('mri,mrj->mij', square_array_operand, square_array_operand, precision=finest_arithmetic_mode)

def newton_steps(mats, combine):
    gram_list = combine(tuple((gram_of(square_array_operand) for square_array_operand in mats)))
    scales = tuple((1.0 / (jnp.sqrt(jnp.einsum('mii->m', gram_matrix)) + 1e-07) for gram_matrix in gram_list))
    current = tuple((square_array_operand * norm_scale[:, None, None] for square_array_operand, norm_scale in zip(mats, scales)))
    gram_list = tuple((gram_matrix * (norm_scale * norm_scale)[:, None, None] for gram_matrix, norm_scale in zip(gram_list, scales)))
    for sweep_index in range(5):
        if sweep_index > 0:
            gram_list = combine(tuple((gram_of(square_array_operand) for square_array_operand in current)))
        current = tuple((poly_first * square_array_operand + jnp.einsum('mri,mij->mrj', square_array_operand, poly_second * gram_matrix + poly_third * jnp.einsum('mij,mjk->mik', gram_matrix, gram_matrix, precision=finest_arithmetic_mode), precision=finest_arithmetic_mode) for square_array_operand, gram_matrix in zip(current, gram_list)))
    return current

def unchanged(gram_list):
    return gram_list

def reference(tokens, cotangent, norm_gain, w_zx, state_proj_weight, step_weight, exit_coefficient_matrix, x_params, bc_params, head_params, zx_moment, bc_moment, dt_moment, out_moment, gain_moment, xpar_moment, bcpar_moment, head_moment):
    params = (norm_gain, w_zx, state_proj_weight, step_weight, exit_coefficient_matrix, x_params, bc_params, head_params)

    def one_sequence(totals, pair_in):
        sequence, upstream = pair_in
        output, pullback = jax.vjp(forward, sequence, *params)
        grads = pullback(upstream)
        return (tuple((left + right for left, right in zip(totals, grads[1:]))), (output.astype(jnp.bfloat16), grads[0]))
    zero_grads = tuple((jnp.zeros_like(param) for param in params))
    grads, (outputs, input_grads) = lax.scan(one_sequence, zero_grads, (tokens.astype(jnp.float32)[:, None], cotangent.astype(jnp.float32)[:, None]))
    result = outputs[:, 0]
    input_grad = input_grads[:, 0]
    gain_g, zx_g, bc_g, dt_g, out_g, xpar_g, bcpar_g, head_g = grads
    zx_m = momentum_rate * zx_moment + zx_g
    bc_m = momentum_rate * bc_moment + bc_g
    dt_m = momentum_rate * dt_moment + dt_g
    out_m = momentum_rate * out_moment + out_g
    mats = to_matrices(zx_g + momentum_rate * zx_m, bc_g + momentum_rate * bc_m, dt_g + momentum_rate * dt_m, out_g + momentum_rate * out_m, P_SIZE)
    zx_ortho, bc_ortho, dt_ortho, out_ortho = from_matrices(*newton_steps(mats, unchanged))
    shrink = 1.0 - matrix_rate * weight_decay
    zx_new = w_zx * shrink - matrix_rate * zx_ortho
    bc_new = state_proj_weight * shrink - matrix_rate * bc_ortho
    dt_new = step_weight * shrink - matrix_rate * dt_ortho
    out_new = exit_coefficient_matrix * shrink - matrix_rate * out_ortho
    gain_m = momentum_rate * gain_moment + gain_g
    xpar_m = momentum_rate * xpar_moment + xpar_g
    bcpar_m = momentum_rate * bcpar_moment + bcpar_g
    head_m = momentum_rate * head_moment + head_g
    gain_new = norm_gain - small_rate * (gain_g + momentum_rate * gain_m)
    xpar_new = x_params - small_rate * (xpar_g + momentum_rate * xpar_m)
    bcpar_new = bc_params - small_rate * (bcpar_g + momentum_rate * bcpar_m)
    head_new = head_params - small_rate * (head_g + momentum_rate * head_m)
    return (result, input_grad, zx_m, zx_new, bc_m, bc_new, dt_m, dt_new, out_m, out_new, gain_m, gain_new, xpar_m, xpar_new, bcpar_m, bcpar_new, head_m, head_new)
```

```python
import functools

import jax
import jax.numpy as jnp
from jax import lax
from jax.experimental import pallas as pl
from jax.experimental.pallas import tpu as pltpu
from jax.sharding import PartitionSpec as P

BF = jnp.bfloat16
F32 = jnp.float32
CHUNK = 128
LANES = 128
ROWS = 256
PIECE = 64
WIDE_ROWS = 512
VMEM_BYTES = 52 * 1024 * 1024

exact = lax.Precision.HIGHEST
norm_eps = 1e-05
poly_first = 3.4445
poly_second = -4.775
poly_third = 2.0315
momentum_rate = 0.95
matrix_rate = 0.5
weight_decay = 0.1
small_rate = 0.0025


def params(count):
    return pltpu.CompilerParams(
        dimension_semantics=("arbitrary",) * count, vmem_limit_bytes=VMEM_BYTES
    )


def cost(flops, moved, transcendentals=0):
    return pl.CostEstimate(
        flops=flops // 40, bytes_accessed=moved // 40, transcendentals=transcendentals // 40
    )


def sigmoid(value):
    return 0.5 * jnp.tanh(0.5 * value) + 0.5


def dot(left, right):
    return jnp.dot(left, right, preferred_element_type=F32)


def dot_nt(left, right):
    return lax.dot_general(left, right, (((1,), (1,)), ((), ())), preferred_element_type=F32)


def halves(value):
    high = value.astype(BF)
    low = (value - high.astype(F32)).astype(BF)
    return high, low


def spread_dot(value, spread):
    high, low = halves(value)
    return dot(jnp.concatenate([high, low], axis=1), spread)


def gather_dot(value, spread):
    high, low = halves(value)
    return dot_nt(high, spread) + dot_nt(low, spread)


def tri_dot(triangle, value):
    first = value.astype(BF)
    rest = value - first.astype(F32)
    second = rest.astype(BF)
    third = (rest - second.astype(F32)).astype(BF)
    return dot(triangle, first) + dot(triangle, second) + dot(triangle, third)


def flip(value):
    return value.astype(F32).T.astype(BF)


def row_fold(value):
    return value.reshape(-1, 8, value.shape[-1]).sum(axis=0)


def tiles_of(start, stop, step):
    return [(low, min(step, stop - low)) for low in range(start, stop, step)]


def iota(shape, axis):
    return lax.broadcasted_iota(jnp.int32, shape, axis)


def project_kernel(
    kwidth, normed, weight, taps, heads, conv_in, bc_pre, conv_x, conv_bc, step, cum, buffer
):
    inner = conv_in.shape[-1]
    states = bc_pre.shape[-1]
    rows = normed.shape[1]
    block = pl.program_id(1)

    @pl.when(block == 0)
    def _():
        buffer[0:8, :] = jnp.zeros((8, inner + states), F32)

    @pl.when(block > 0)
    def _():
        buffer[0:8, :] = buffer[rows : rows + 8, :]

    data = normed[0]
    for low, width in tiles_of(0, inner, 256) + tiles_of(inner, inner + states, 256):
        cols = slice(low, low + width)
        made = dot(data, weight[:, cols])
        buffer[8 : 8 + rows, cols] = made
        for top in range(0, rows, PIECE):
            for left in range(low, low + width, LANES):
                here = slice(left, left + LANES)
                kept = buffer[8 + top : 8 + top + PIECE, here]
                total = taps[kwidth : kwidth + 1, here] + taps[kwidth - 1 : kwidth, here] * kept
                for offset in range(kwidth - 1):
                    start = 9 - kwidth + offset + top
                    total = total + taps[offset : offset + 1, here] * (
                        buffer[start : start + PIECE, here]
                    )
                active = (total * sigmoid(total)).astype(BF)
                span = slice(top, top + PIECE)
                if left < inner:
                    conv_in[0, span, here] = kept.astype(BF)
                    conv_x[0, span, here] = active
                else:
                    own = slice(left - inner, left - inner + LANES)
                    bc_pre[0, span, own] = kept
                    conv_bc[0, span, own] = active
    delta = dot(data, weight[:, inner + states :]) + heads[1:2, :]
    size = jnp.maximum(delta, 0.0) + jnp.log1p(jnp.exp(-jnp.abs(delta)))
    decay = -size * jnp.exp(heads[0:1, :])
    step[0] = size
    lower = (iota((CHUNK, CHUNK), 0) >= iota((CHUNK, CHUNK), 1)).astype(F32).astype(BF)
    for low in range(0, rows, CHUNK):
        cum[0, low : low + CHUNK, :] = tri_dot(lower, decay[low : low + CHUNK, :])


def scan_kernel(conv_x, conv_bc, step, cum, spread2, skip, y, states, state):
    inner = conv_x.shape[-1]
    width = conv_bc.shape[-1] // 2
    state[...] = jnp.zeros_like(state)
    causal = iota((CHUNK, CHUNK), 0) >= iota((CHUNK, CHUNK), 1)
    first = iota((CHUNK, LANES), 1) < LANES // 2
    spread = spread2[...]

    def body(index, carry):
        rows = pl.ds(pl.multiple_of(index * CHUNK, CHUNK), CHUNK)
        value = conv_x[0, rows, :]
        b_part = conv_bc[0, rows, :width]
        c_part = conv_bc[0, rows, width:]
        running = cum[0, rows, :]
        size = step[0, rows, :]
        state_low = state[...].astype(BF)
        states[0, index] = state_low
        scores = dot_nt(c_part, b_part)
        carried = dot(c_part, state_low)
        grow = spread_dot(jnp.exp(running), spread)
        tail = spread_dot(size * jnp.exp(running[CHUNK - 1 : CHUNK, :] - running), spread)
        keys = (running - jnp.log(size)).T
        for pair in range(inner // LANES):
            cols = slice(pair * LANES, (pair + 1) * LANES)
            pair_x = value[:, cols]
            parts = []
            for head in (2 * pair, 2 * pair + 1):
                gap = running[:, head : head + 1] - keys[head : head + 1, :]
                kernel = jnp.where(causal, jnp.exp(gap) * scores, 0.0).astype(BF)
                parts.append(dot(kernel, pair_x))
            y[0, rows, cols] = (
                jnp.where(first, parts[0], parts[1])
                + carried[:, cols] * grow[:, cols]
                + skip[0:1, cols] * pair_x.astype(F32)
            )
        weighted = (value.astype(F32) * tail).astype(BF)
        state[...] = state[...] * grow[CHUNK - 1 : CHUNK, :] + dot(flip(b_part), weighted)
        return carry

    lax.fori_loop(0, conv_x.shape[1] // CHUNK, body, 0)


def gate_kernel(normed, cotangent, weight, y, gain, gate_pre, grad_mixed, stats):
    inner = y.shape[-1]
    rows = normed.shape[1]
    data = normed[0]
    upstream = cotangent[0]
    squares = [jnp.zeros((PIECE, LANES), F32) for _ in range(rows // PIECE)]
    products = [jnp.zeros((PIECE, LANES), F32) for _ in range(rows // PIECE)]
    for low, width in tiles_of(0, inner, 256):
        cols = slice(low, low + width)
        pre_all = dot(data, weight[:, cols])
        grad_all = dot(upstream, weight[:, inner + low : inner + low + width])
        gate_pre[0, :, cols] = pre_all.astype(BF)
        grad_mixed[0, :, cols] = grad_all.astype(BF)
        for piece in range(rows // PIECE):
            span = slice(piece * PIECE, (piece + 1) * PIECE)
            for left in range(0, width, LANES):
                here = slice(low + left, low + left + LANES)
                pre = pre_all[span, left : left + LANES]
                gated = y[0, span, here] * pre * sigmoid(pre)
                squares[piece] = squares[piece] + gated * gated
                products[piece] = products[piece] + (
                    grad_all[span, left : left + LANES] * gain[0:1, here] * gated
                )
    squares = jnp.concatenate(squares, axis=0)
    products = jnp.concatenate(products, axis=0)
    lane = iota((rows, LANES), 1)
    both = jnp.where(
        lane == 0,
        jnp.sum(squares, axis=1, keepdims=True),
        jnp.where(lane == 1, jnp.sum(products, axis=1, keepdims=True), 0.0),
    )
    stats[0] = both.T[0:8, :]


def mix_kernel(
    starts,
    y,
    gate_pre,
    grad_mixed,
    scales,
    gain,
    weight,
    mixed,
    grad_y,
    grad_gate,
    own_core,
    other_core,
    gain_sum,
):
    inner = y.shape[-1]
    rows = y.shape[1]

    @pl.when((pl.program_id(0) == 0) & (pl.program_id(1) == 0))
    def _():
        gain_sum[...] = jnp.zeros_like(gain_sum)

    by_row = scales[0].T
    inverse = by_row[:, 0:1]
    slope = by_row[:, 1:2]
    for low in range(0, inner, LANES):
        cols = slice(low, low + LANES)
        gain_here = gain[0:1, cols]
        folded = jnp.zeros((8, LANES), F32)
        for top in range(0, rows, PIECE):
            span = slice(top, top + PIECE)
            value = y[0, span, cols]
            pre = gate_pre[0, span, cols].astype(F32)
            upstream = grad_mixed[0, span, cols].astype(F32)
            logistic = sigmoid(pre)
            act = pre * logistic
            gated = value * act
            scaled = gated * inverse[span]
            folded = folded + row_fold(upstream * scaled)
            mixed[0, span, cols] = (scaled * gain_here).astype(BF)
            grad_gated = inverse[span] * (upstream * gain_here) - gated * slope[span]
            grad_y[0, span, cols] = (grad_gated * act).astype(BF)
            grad_gate[0, span, cols] = (
                grad_gated * value * (logistic * (1.0 + pre * (1.0 - logistic)))
            ).astype(BF)
        gain_sum[:, cols] += folded
    data = mixed[0]
    share = own_core.shape[-1]
    columns = own_core.shape[0]
    for part in range(2 * columns):
        rows = pl.ds(pl.multiple_of(starts[part], share), share)
        made = dot_nt(data, weight[rows, :]).astype(BF)
        if part < columns:
            own_core[part, 0] = made
        else:
            other_core[part - columns, 0] = made


def back_kernel(
    kwidth,
    conv_x,
    conv_bc,
    step,
    cum,
    grad_y,
    y,
    states,
    conv_in,
    taps,
    heads,
    spread1,
    spread2,
    skip,
    in_before,
    old_taps,
    old_heads,
    after_in,
    after_bc,
    after_delta,
    grad_in,
    grad_bc,
    grad_delta,
    tap_sums,
    head_sums,
    grad_state,
    back_buffer,
    in_buffer,
):
    inner = conv_x.shape[-1]
    width = conv_bc.shape[-1] // 2
    chunks = conv_x.shape[1] // CHUNK
    step_index = pl.program_id(0)
    first_block = step_index == pl.num_programs(0) - 1

    @pl.when(step_index == 0)
    def _():
        tap_sums[...] = old_taps[...]
        head_sums[...] = old_heads[...]
        grad_state[...] = jnp.zeros_like(grad_state)
        back_buffer[0:8, :] = jnp.zeros((8, inner), F32)

    anti = iota((CHUNK, CHUNK), 0) <= iota((CHUNK, CHUNK), 1)
    upper = anti.astype(F32).astype(BF)
    first = iota((CHUNK, LANES), 1) < LANES // 2
    rate = jnp.exp(heads[0:1, :])
    spread = spread2[...]
    gather = spread1[...]

    for index in reversed(range(chunks)):
        rows = slice(index * CHUNK, (index + 1) * CHUNK)
        value = conv_x[0, rows, :]
        b_part = conv_bc[0, rows, :width]
        c_part = conv_bc[0, rows, width:]
        running = cum[0, rows, :]
        size = step[0, rows, :]
        upstream = grad_y[0, rows, :]
        old_state = states[0, index]
        state_grad = grad_state[...]
        state_grad_low = state_grad.astype(BF)
        scores = dot_nt(b_part, c_part)
        reach = dot(b_part, state_grad_low)
        grow = spread_dot(jnp.exp(running), spread)
        tail = spread_dot(size * jnp.exp(running[CHUNK - 1 : CHUNK, :] - running), spread)
        grown = (upstream.astype(F32) * grow).astype(BF)
        weighted = (value.astype(F32) * tail).astype(BF)
        grad_c = dot_nt(grown, old_state)
        grad_b = dot_nt(weighted, state_grad_low)
        last_grow = grow[CHUNK - 1 : CHUNK, :]
        grad_state[...] = state_grad * last_grow + dot(flip(c_part), grown)
        kept = row_fold(old_state.astype(F32) * state_grad) * last_grow
        queries = running.T
        keys = running - jnp.log(size)
        score_grad = jnp.zeros((CHUNK, CHUNK), F32)
        flow_parts = []
        pull_parts = []
        end_parts = []
        if index > 0:
            in_buffer[0:16, :] = conv_in[0, index * CHUNK - 16 : index * CHUNK, :].astype(F32)
        else:
            in_buffer[0:16, :] = jnp.where(first_block, 0.0, in_before[0].astype(F32))
        in_buffer[16 : 16 + CHUNK, :] = conv_in[0, rows, :].astype(F32)
        back_buffer[CHUNK : CHUNK + 8, :] = back_buffer[0:8, :]
        for pair in range(inner // LANES):
            cols = slice(pair * LANES, (pair + 1) * LANES)
            pair_x = value[:, cols]
            pair_up = upstream[:, cols]
            parts = []
            for side in (0, 1):
                head = 2 * pair + side
                gap = queries[head : head + 1, :] - keys[:, head : head + 1]
                kernel = jnp.where(anti, jnp.exp(gap), 0.0)
                own_x = jnp.where(first if side == 0 else ~first, pair_x, jnp.zeros_like(pair_x))
                score_grad = score_grad + kernel * dot_nt(own_x, pair_up)
                parts.append(dot((kernel * scores).astype(BF), pair_up))
            x_wide = pair_x.astype(F32)
            up_wide = pair_up.astype(F32)
            far = reach[:, cols] * tail[:, cols]
            inside = jnp.where(first, parts[0], parts[1]) + far
            skip_row = skip[0:1, cols]
            pull = x_wide * inside
            pull_parts.append(pull)
            flow_parts.append(up_wide * (y[0, rows, cols] - skip_row * x_wide) - pull)
            end_parts.append(row_fold(x_wide * far) + kept[:, cols])
            grad_x = inside + skip_row * up_wide
            now = in_buffer[16 : 16 + CHUNK, cols]
            shifted = [
                in_buffer[17 - kwidth + offset : 17 - kwidth + offset + CHUNK, cols]
                for offset in range(kwidth - 1)
            ] + [now]
            total = taps[kwidth : kwidth + 1, cols]
            for offset in range(kwidth):
                total = total + taps[offset : offset + 1, cols] * shifted[offset]
            logistic = sigmoid(total)
            error = grad_x * (logistic * (1.0 + total * (1.0 - logistic)))
            back_buffer[0:CHUNK, cols] = error
            for offset in range(kwidth):
                tap_sums[8 * offset : 8 * offset + 8, cols] += row_fold(error * shifted[offset])
            tap_sums[8 * kwidth : 8 * kwidth + 8, cols] += row_fold(error)
            tap_sums[8 * kwidth + 8 : 8 * kwidth + 16, cols] += row_fold(x_wide * up_wide)
            moved = taps[kwidth - 1 : kwidth, cols] * error
            for offset in range(kwidth - 1):
                start = kwidth - 1 - offset
                moved = moved + (
                    taps[offset : offset + 1, cols] * back_buffer[start : start + CHUNK, cols]
                )
            grad_in[0, rows, cols] = moved.astype(BF)
        score_low = score_grad.astype(BF)
        grad_bc[0, rows, :width] = (grad_b + dot(score_low, c_part)).astype(BF)
        grad_bc[0, rows, width:] = (grad_c + dot(flip(score_grad), b_part)).astype(BF)
        flow = gather_dot(jnp.concatenate(flow_parts, axis=1), gather)
        pull = gather_dot(jnp.concatenate(pull_parts, axis=1), gather)
        ends = gather_dot(jnp.concatenate(end_parts, axis=1), gather)
        decay_grad = tri_dot(upper, flow) + jnp.sum(ends, axis=0, keepdims=True)
        size_grad = pull / jnp.maximum(size, 1e-37) - rate * decay_grad
        small = size * (1.0 - size * (0.5 - size * (1.0 / 6.0)))
        delta_grad = size_grad * jnp.where(size < 0.01, small, 1.0 - jnp.exp(-size))
        grad_delta[0, rows, :] = delta_grad.astype(BF)
        head_sums[0:8, :] += row_fold(decay_grad * (-size * rate))
        head_sums[8:16, :] += row_fold(delta_grad)


def join_kernel(
    starts, grad_gate, grad_in, grad_delta, gate_weight, in_weight, step_weight, own_core, other_core
):
    share = own_core.shape[-1]
    columns = own_core.shape[0]
    for part in range(2 * columns):
        rows = pl.ds(pl.multiple_of(starts[part], share), share)
        total = dot_nt(grad_gate[0], gate_weight[rows, :])
        total = total + dot_nt(grad_in[0], in_weight[rows, :])
        total = total + dot_nt(grad_delta[0], step_weight[rows, :])
        if part < columns:
            own_core[part, 0] = total.astype(BF)
        else:
            other_core[part - columns, 0] = total.astype(BF)


def bc_kernel(kwidth, summed, pre, taps, grad_delta, grad_small, tap_sums, before, later):
    length = pre.shape[1]
    width = pre.shape[2]

    @pl.when(pl.program_id(0) == 0)
    def _():
        tap_sums[...] = jnp.zeros_like(tap_sums)

    before[0:8, :] = jnp.zeros((8, width), F32)
    before[8 : 8 + length, :] = pre[0]
    later[length : length + 8, :] = jnp.zeros((8, width), F32)
    for left in range(0, width, LANES):
        here = slice(left, left + LANES)

        folds = [jnp.zeros((8, LANES), F32) for _ in range(kwidth + 1)]
        for top in range(0, length, PIECE):
            span = slice(top, top + PIECE)
            shifted = [
                before[top + 9 - kwidth + offset : top + 9 - kwidth + offset + PIECE, here]
                for offset in range(kwidth)
            ]
            total = taps[kwidth : kwidth + 1, here]
            for offset in range(kwidth):
                total = total + taps[offset : offset + 1, here] * shifted[offset]
            logistic = sigmoid(total)
            error = summed[0, span, here].astype(F32) * (
                logistic * (1.0 + total * (1.0 - logistic))
            )
            later[span, here] = error
            for offset in range(kwidth):
                folds[offset] = folds[offset] + row_fold(error * shifted[offset])
            folds[kwidth] = folds[kwidth] + row_fold(error)
        for offset in range(kwidth + 1):
            tap_sums[8 * offset : 8 * offset + 8, here] += folds[offset]
        for top in range(0, length, PIECE):
            moved = taps[kwidth - 1 : kwidth, here] * later[top : top + PIECE, here]
            for offset in range(kwidth - 1):
                start = top + kwidth - 1 - offset
                moved = moved + taps[offset : offset + 1, here] * later[start : start + PIECE, here]
            grad_small[0, top : top + PIECE, here] = moved.astype(BF)
    grad_small[0, :, width:] = grad_delta[0]


def block_mask():
    half = LANES // 2
    return (iota((LANES, LANES), 0) < half) == (iota((LANES, LANES), 1) < half)


def pair_pack(matrix):
    half = LANES // 2
    return jnp.where(iota((half, LANES), 1) < half, matrix[:half], matrix[half:])


def pair_unpack(unit):
    half = LANES // 2
    left = iota((half, LANES), 1) < half
    return jnp.concatenate([jnp.where(left, unit, 0.0), jnp.where(left, 0.0, unit)], axis=0)


def gram_kernel(slots, first, second, squares, units):
    half = LANES // 2
    pairs, wholes, single = slots
    units[...] = jnp.zeros_like(units)
    split = first.shape[1] // LANES
    for index in range(pairs + len(wholes)):
        source, at = (first, index) if index < split else (second, index - split)
        part = source[:, at * LANES : (at + 1) * LANES]
        made = jnp.dot(part.T, part, precision=exact, preferred_element_type=F32)
        if index < pairs:
            units[index] = pair_pack(made)
        else:
            slot = wholes[index - pairs]
            units[slot] = made[:half]
            units[slot + 1] = made[half:]
    units[single, 0:8, :] = squares[...]


def newton_kernel(parts, kinds, result):
    half = LANES // 2
    same = block_mask()
    eye = (iota((LANES, LANES), 0) == iota((LANES, LANES), 1)).astype(F32)
    low_row = iota((LANES, 1), 0) < half
    low_col = iota((1, LANES), 1) < half

    def mul(left, right):
        return jnp.dot(left, right, precision=exact, preferred_element_type=F32)

    count = result.shape[0]
    sums = []
    for index in range(count):
        total = parts[0, index]
        for source in range(1, parts.shape[0]):
            total = total + parts[source, index]
        sums.append(total)
    whole = kinds[0:1, :] > 0.5
    is_whole = whole[:, 0:1]
    grams = [pair_unpack(unit) for unit in sums]
    grams[0] = jnp.where(whole, jnp.concatenate(sums[:2], axis=0), grams[0])
    scales = []
    for index in range(count):
        diagonal = jnp.sum(grams[index] * eye, axis=0, keepdims=True)
        low_trace = jnp.sum(jnp.where(low_col, diagonal, 0.0), axis=1, keepdims=True)
        high_trace = jnp.sum(jnp.where(low_col, 0.0, diagonal), axis=1, keepdims=True)
        if index == 0:
            both = low_trace + high_trace
            low_trace = jnp.where(is_whole, both, low_trace)
            high_trace = jnp.where(is_whole, both, high_trace)
        low_scale = 1.0 / (jnp.sqrt(low_trace) + 1e-07)
        high_scale = 1.0 / (jnp.sqrt(high_trace) + 1e-07)
        scale_row = jnp.where(low_row, low_scale, high_scale)
        scale_col = jnp.where(low_col, low_scale, high_scale)
        grams[index] = grams[index] * scale_row * scale_col
        scales.append(scale_row)
    totals = [None] * count
    for sweep in range(5):
        squares = [mul(gram, gram) for gram in grams]
        factors = [
            poly_first * eye + poly_second * gram + poly_third * square
            for gram, square in zip(grams, squares)
        ]
        totals = [
            scale * factor if sweep == 0 else mul(total, factor)
            for scale, total, factor in zip(scales, totals, factors)
        ]
        if sweep < 4:
            halfway = [mul(factor, gram) for factor, gram in zip(factors, grams)]
            grams = [mul(left, factor) for left, factor in zip(halfway, factors)]
    for index in range(count):
        made = pair_pack(totals[index])
        if index < 2:
            here = totals[0][:half] if index == 0 else totals[0][half:]
            made = jnp.where(whole, here, made)
        length = sums[index]
        scale = 1.0 / (jnp.sqrt(length) + 1e-07)
        length = length * scale * scale
        for sweep in range(5):
            step = poly_first + length * (poly_second + poly_third * length)
            scale = scale * step
            length = length * step * step
        single = kinds[8 + index : 9 + index, :] > 0.5
        result[index] = jnp.where(single, scale, made).astype(BF)


def apply_kernel(slots, first, second, units, made):
    pairs, wholes, single = slots
    split = first.shape[1] // LANES
    for index in range(pairs + len(wholes)):
        source, at = (first, index) if index < split else (second, index - split)
        if index < pairs:
            factor = pair_unpack(units[index].astype(F32))
        else:
            slot = wholes[index - pairs]
            factor = jnp.concatenate([units[slot], units[slot + 1]], axis=0).astype(F32)
        made[:, index * LANES : (index + 1) * LANES] = jnp.dot(
            source[:, at * LANES : (at + 1) * LANES],
            factor,
            precision=exact,
            preferred_element_type=F32,
        )


def whole_call(kernel, shapes, *operands):
    return pl.pallas_call(
        kernel,
        out_shape=shapes,
        compiler_params=pltpu.CompilerParams(vmem_limit_bytes=VMEM_BYTES),
    )(*operands)


def seen(shape, dtype=F32):
    return jax.ShapeDtypeStruct(shape, dtype)


def by_rows(width, rows=WIDE_ROWS):
    return pl.BlockSpec((1, rows, width), lambda s, t: (s, t, 0))


def fixed(shape, count):
    if count == 2:
        return pl.BlockSpec(shape, lambda s, t: (0,) * len(shape))
    return pl.BlockSpec(shape, lambda s: (0,) * len(shape))


def pad_rows(array, rows=8):
    return jnp.pad(array, ((0, rows - array.shape[0]), (0, 0)))


def pad_cols(array, cols):
    return jnp.pad(array, ((0, 0), (0, cols - array.shape[1])))


def copy_to_all(array, axis):
    count = lax.axis_size(axis)
    return lax.all_to_all(
        jnp.broadcast_to(array, (count,) + array.shape), axis, split_axis=0, concat_axis=0, tiled=True
    )


def block_starts(share):
    columns = lax.axis_size("tensor") // 2
    me = lax.axis_index("tensor")
    order = (me // 2 + jnp.arange(columns)) % columns
    return (
        share * jnp.concatenate([2 * order + me % 2, 2 * order + 1 - me % 2])
    ).astype(jnp.int32)


def core_sums(own, arrived):
    kept = own[0].astype(F32) + arrived[0].astype(F32)
    leaving = [
        (own[shift].astype(F32) + arrived[shift].astype(F32)).astype(BF)
        for shift in range(1, own.shape[0])
    ]
    return kept, leaving


def core_phase(own, other):
    count = lax.axis_size("tensor")
    return core_sums(own, lax.ppermute(other, "tensor", [(i, i ^ 1) for i in range(count)]))


def column_sends(leaving):
    count = lax.axis_size("tensor")
    columns = count // 2
    return [
        lax.ppermute(
            sent,
            "tensor",
            [(i, ((i // 2 + shift) % columns) * 2 + i % 2) for i in range(count)],
        )
        for shift, sent in enumerate(leaving, 1)
    ]


def column_phase(kept, leaving):
    for moved in column_sends(leaving):
        kept = kept + moved.astype(F32)
    return kept


def tensor_sum(value):
    count = lax.axis_size("tensor")
    step = 1
    while step < count:
        value = value + lax.ppermute(value, "tensor", [(i, i ^ step) for i in range(count)])
        step *= 2
    return value


def after(value, *others):
    return lax.optimization_barrier((value,) + others)[0]


def tie(*values):
    return lax.optimization_barrier(values)


def gather_rows(shard):
    count = lax.axis_size("dp")
    if count != 8:
        return lax.all_gather(shard, "dp", axis=0, tiled=True), shard, shard
    rows = shard.shape[0]
    me = lax.axis_index("dp")
    z = me // 2
    y = me % 2
    result = jnp.zeros((9 * rows, shard.shape[1]), shard.dtype)
    swap = [(i, i ^ 1) for i in range(count)]

    def place(result, piece, z_from, y_from):
        there = (z_from >= 0) & (z_from < 4)
        start = jnp.where(there, (z_from * 2 + y_from) * rows, 8 * rows)
        return lax.dynamic_update_slice_in_dim(result, piece, start, 0)

    other = lax.ppermute(shard, "dp", swap)
    result = place(result, shard, z, y)
    up = down = shard
    for step in range(1, 4):
        up = lax.ppermute(
            up, "dp", [(2 * i + j, 2 * i + 2 + j) for i in range(step - 1, 3) for j in range(2)]
        )
        down = lax.ppermute(
            down, "dp", [(2 * i + j, 2 * i - 2 + j) for i in range(1, 5 - step) for j in range(2)]
        )
        result = place(place(result, up, z - step, y), down, z + step, y)
    leaving = jnp.concatenate(
        [
            lax.dynamic_slice_in_dim(result, ((z ^ k) * 2 + y) * rows, rows, 0)
            for k in range(1, 4)
        ],
        axis=0,
    )
    arrived = lax.ppermute(leaving, "dp", swap)
    result = place(result, other, z, 1 - y)
    for k in range(1, 4):
        result = place(result, arrived[(k - 1) * rows : k * rows], z ^ k, 1 - y)
    return result, up, down


def sum_parts(parts):
    count = lax.axis_size("dp")
    return parts.reshape(count, -1, parts.shape[1]).astype(F32).sum(axis=0)


def add_low(left, right):
    return (left.astype(F32) + right.astype(F32)).astype(BF)


def chip_total(value):
    count = lax.axis_size("tensor")
    half = value.shape[1] // 2
    arrived = lax.ppermute(value, "tensor", [(i, i ^ 1) for i in range(count)])
    start = lax.axis_index("tensor") % 2 * half
    return add_low(
        lax.dynamic_slice_in_dim(value, start, half, 1),
        lax.dynamic_slice_in_dim(arrived, start, half, 1),
    )


def column_total_sends(part):
    count = lax.axis_size("tensor")
    return lax.ppermute(part, "tensor", [(i, i ^ 2) for i in range(count)])


def finish_total(part, moved):
    count = lax.axis_size("tensor")
    part = add_low(part, moved)
    step = 4
    while step < count:
        part = add_low(part, lax.ppermute(part, "tensor", [(i, i ^ step) for i in range(count)]))
        step *= 2
    other = lax.ppermute(part, "tensor", [(i, i ^ 1) for i in range(count)])
    first = lax.axis_index("tensor") % 2 == 0
    return jnp.concatenate(
        [jnp.where(first, part, other), jnp.where(first, other, part)], axis=1
    )


def dp_sum(value):
    count = lax.axis_size("dp")
    step = 1
    while step < count:
        value = value + lax.ppermute(value, "dp", [(i, i ^ step) for i in range(count)])
        step *= 2
    return value


def gram_units(first, second, squares):
    dp = lax.axis_size("dp")
    half = LANES // 2
    pairs = (first.shape[1] + second.shape[1]) // LANES - 2
    each = max(2, -(-pairs // (dp - 2)))
    wholes = ((dp - 2) * each, (dp - 1) * each)
    single = wholes[0] + 2 if each > 2 else wholes[0] - each
    slots = (pairs, wholes, single)
    square_rows = pad_rows(pad_cols(squares[None], LANES))
    units = whole_call(
        functools.partial(gram_kernel, slots),
        seen((dp * each, half, LANES)),
        first,
        second,
        square_rows,
    )
    return units, slots


def orthogonal(first, second, units, slots, count):
    dp = lax.axis_size("dp")
    half = LANES // 2
    each = units.shape[0] // dp
    single = slots[2]
    parts = lax.all_to_all(units, "dp", split_axis=0, concat_axis=0, tiled=True)
    me = lax.axis_index("dp")
    kinds = jnp.concatenate(
        [
            jnp.broadcast_to((me >= dp - 2).astype(F32), (8, LANES)),
            jnp.broadcast_to(
                (me * each + jnp.arange(8) == single).astype(F32)[:, None], (8, LANES)
            ),
        ],
        axis=0,
    )
    factors = whole_call(
        newton_kernel, seen((each, half, LANES), BF), parts.reshape(dp, each, half, LANES), kinds
    )
    factors = copy_to_all(factors, "dp").reshape(dp * each, half, LANES)
    made = whole_call(
        functools.partial(apply_kernel, slots),
        seen((first.shape[0], first.shape[1] + second.shape[1])),
        first,
        second,
        factors,
    )
    return made, factors[single, 0, :count].astype(F32)


def local(
    tokens,
    cotangent,
    norm_gain,
    w_zx,
    state_proj_weight,
    step_weight,
    exit_coefficient_matrix,
    x_params,
    bc_params,
    head_params,
    zx_moment,
    bc_moment,
    dt_moment,
    out_moment,
    gain_moment,
    xpar_moment,
    bcpar_moment,
    head_moment,
):
    kwidth = bc_params.shape[0] - 1
    heads = head_params.shape[1]
    inner = x_params.shape[1]
    head_width = inner // heads
    states = bc_params.shape[1]
    seqs, length, model = tokens.shape
    tensor = lax.axis_size("tensor")
    tensor_index = lax.axis_index("tensor")
    share = model // tensor
    share_start = tensor_index * share
    whole_inner = inner * tensor
    blocks = length // ROWS
    wide_blocks = length // WIDE_ROWS
    chunks = length // CHUNK
    tokens_here = seqs * length

    first_weight, last_up, last_down = gather_rows(
        jnp.concatenate(
            [w_zx[:, 1, :], state_proj_weight, pad_cols(step_weight, LANES)], axis=1
        ).astype(BF)
    )
    second_part = jnp.concatenate([w_zx[:, 0, :], exit_coefficient_matrix.T], axis=1).astype(BF)
    second_weight = lax.all_gather(
        after(second_part, last_up, last_down), "dp", axis=0, tiled=True
    )
    wide = after(tokens, last_up, last_down, second_part).astype(F32)
    inv_rms = lax.rsqrt(jnp.mean(wide * wide, axis=-1, keepdims=True) + norm_eps)
    normed = lax.optimization_barrier((wide * inv_rms * norm_gain).astype(BF))
    any_spec = pl.BlockSpec(memory_space=pl.ANY)

    starts = block_starts(share)

    taps = pad_rows(jnp.concatenate([x_params[: kwidth + 1], bc_params], axis=1))
    head_rows = pad_rows(pad_cols(head_params, LANES))
    lane_head = jnp.arange(inner) // head_width
    spread1 = (jnp.arange(LANES)[:, None] == lane_head[None, :]).astype(BF)
    spread2 = jnp.concatenate([spread1, spread1], axis=0)
    skip_row = jnp.broadcast_to(jnp.repeat(head_params[2], head_width)[None], (8, inner))
    gain_row = jnp.broadcast_to(x_params[kwidth + 1][None], (8, inner))

    first_cols = first_weight.shape[1]
    conv_in, bc_pre, conv_x, conv_bc, step, cum = pl.pallas_call(
        functools.partial(project_kernel, kwidth),
        grid=(seqs, wide_blocks),
        in_specs=[
            by_rows(model),
            fixed((model, first_cols), 2),
            fixed((8, inner + states), 2),
            fixed((8, LANES), 2),
        ],
        out_specs=[
            by_rows(inner),
            by_rows(states),
            by_rows(inner),
            by_rows(states),
            by_rows(LANES),
            by_rows(LANES),
        ],
        out_shape=[
            seen((seqs, length, inner), BF),
            seen((seqs, length, states)),
            seen((seqs, length, inner), BF),
            seen((seqs, length, states), BF),
            seen((seqs, length, LANES)),
            seen((seqs, length, LANES)),
        ],
        scratch_shapes=[pltpu.VMEM((WIDE_ROWS + 8, inner + states), F32)],
        compiler_params=params(2),
        cost_estimate=cost(
            28 * 10**9, tokens_here * (model + 3 * inner) * 2
        ),
        name="project",
    )(normed, first_weight, taps, head_rows)

    def per_seq(width):
        return pl.BlockSpec((1, length, width), lambda s: (s, 0, 0))

    state_spec = pl.BlockSpec((1, chunks, states // 2, inner), lambda s: (s, 0, 0, 0))
    mixed_y, old_states = pl.pallas_call(
        scan_kernel,
        grid=(seqs,),
        in_specs=[
            per_seq(inner),
            per_seq(states),
            per_seq(LANES),
            per_seq(LANES),
            fixed((2 * LANES, inner), 1),
            fixed((8, inner), 1),
        ],
        out_specs=[per_seq(inner), state_spec],
        out_shape=[
            seen((seqs, length, inner)),
            seen((seqs, chunks, states // 2, inner), BF),
        ],
        scratch_shapes=[pltpu.VMEM((states // 2, inner), F32)],
        compiler_params=params(1),
        cost_estimate=cost(
            20 * 10**9, tokens_here * inner * 8, tokens_here * heads * CHUNK
        ),
        name="scan",
    )(conv_x, conv_bc, step, cum, spread2, skip_row)

    stats_spec = pl.BlockSpec((1, 8, WIDE_ROWS), lambda s, t: (s, 0, t))
    gate_pre, grad_mixed, stats = pl.pallas_call(
        gate_kernel,
        grid=(seqs, wide_blocks),
        in_specs=[
            by_rows(model),
            by_rows(model),
            fixed((model, 2 * inner), 2),
            by_rows(inner),
            fixed((8, inner), 2),
        ],
        out_specs=[by_rows(inner), by_rows(inner), stats_spec],
        out_shape=[
            seen((seqs, length, inner), BF),
            seen((seqs, length, inner), BF),
            seen((seqs, 8, length)),
        ],
        compiler_params=params(2),
        cost_estimate=cost(27 * 10**9, tokens_here * (4 * model + 8 * inner)),
        name="gate",
    )(normed, cotangent, second_weight, mixed_y, gain_row)

    sums = tensor_sum(stats[:, :2])
    inverse = lax.rsqrt(sums[:, 0] / whole_inner + norm_eps)
    slope = inverse**3 * (sums[:, 1] / whole_inner)
    scales = jnp.pad(jnp.stack([inverse, slope], axis=1), ((0, 0), (0, 6), (0, 0)))

    columns = tensor // 2
    partial_spec = pl.BlockSpec((columns, 1, WIDE_ROWS, share), lambda s, t: (0, s, t, 0))
    scalar_spec = pl.BlockSpec(memory_space=pltpu.SMEM)
    blended, grad_y, grad_gate, out_own, out_other, gain_fold = pl.pallas_call(
        mix_kernel,
        grid=(seqs, wide_blocks),
        in_specs=[
            scalar_spec,
            by_rows(inner),
            by_rows(inner),
            by_rows(inner),
            stats_spec,
            fixed((8, inner), 2),
            pl.BlockSpec((model, inner), lambda s, t: (0, 1)),
        ],
        out_specs=[
            by_rows(inner),
            by_rows(inner),
            by_rows(inner),
            partial_spec,
            partial_spec,
            fixed((8, inner), 2),
        ],
        out_shape=[
            seen((seqs, length, inner), BF),
            seen((seqs, length, inner), BF),
            seen((seqs, length, inner), BF),
            seen((columns, seqs, length, share), BF),
            seen((columns, seqs, length, share), BF),
            seen((8, inner)),
        ],
        compiler_params=params(2),
        cost_estimate=cost(
            28 * 10**9, tokens_here * (2 * model + 14 * inner)
        ),
        name="mix",
    )(starts, mixed_y, gate_pre, grad_mixed, scales, gain_row, second_weight)

    inputs_share = lax.dynamic_slice_in_dim(tokens, share_start, share, 2).astype(F32)

    def weight_grad(left, right):
        return jnp.einsum("std,stu->du", left, right, preferred_element_type=F32)

    out_grad = weight_grad(cotangent, blended).astype(BF)
    grad_gate, out_grad = tie(grad_gate, out_grad)
    gate_grad = weight_grad(normed, grad_gate).astype(BF)
    early_grad = jnp.concatenate([gate_grad, out_grad], axis=1)
    grad_y, early_grad = tie(grad_y, early_grad)
    early_share = lax.psum_scatter(early_grad, "dp", scatter_dimension=0, tiled=True)

    def back(seq, upstream, old):
        def rows_of(width, rows=ROWS):
            return pl.BlockSpec((1, rows, width), lambda i: (seq, blocks - 1 - i, 0))

        per_block = chunks // blocks
        before_spec = pl.BlockSpec(
            (1, 16, inner),
            lambda i: (seq, jnp.maximum((blocks - 1 - i) * (ROWS // 16) - 1, 0), 0),
        )
        shapes = [
            seen((seqs, length, inner), BF),
            seen((seqs, length, states), BF),
            seen((seqs, length, LANES), BF),
            seen((8 * kwidth + 16, inner)),
            seen((16, LANES)),
        ]
        if old is None:
            in_place = (grad_y, conv_bc, step)
            sums = (jnp.zeros(shapes[3].shape, F32), jnp.zeros(shapes[4].shape, F32))
            aliases = {}
        else:
            in_place = old[:3]
            sums = old[3:]
            aliases = {14: 3, 15: 4, 16: 0, 17: 1, 18: 2}
        return pl.pallas_call(
            functools.partial(back_kernel, kwidth),
            grid=(blocks,),
            in_specs=[
                rows_of(inner),
                rows_of(states),
                rows_of(LANES),
                rows_of(LANES),
                rows_of(inner),
                rows_of(inner),
                pl.BlockSpec(
                    (1, per_block, states // 2, inner), lambda i: (seq, blocks - 1 - i, 0, 0)
                ),
                rows_of(inner),
                fixed((8, inner), 1),
                fixed((8, LANES), 1),
                fixed((LANES, inner), 1),
                fixed((2 * LANES, inner), 1),
                fixed((8, inner), 1),
                before_spec,
                fixed(shapes[3].shape, 1),
                fixed(shapes[4].shape, 1),
                any_spec,
                any_spec,
                any_spec,
            ],
            out_specs=[
                rows_of(inner),
                rows_of(states),
                rows_of(LANES),
                fixed(shapes[3].shape, 1),
                fixed(shapes[4].shape, 1),
            ],
            out_shape=shapes,
            scratch_shapes=[
                pltpu.VMEM((states // 2, inner), F32),
                pltpu.VMEM((CHUNK + 8, inner), F32),
                pltpu.VMEM((CHUNK + 16, inner), F32),
            ],
            input_output_aliases=aliases,
            compiler_params=params(1),
            cost_estimate=cost(25 * 10**9, length * inner * 16, length * heads * CHUNK),
            name="back",
        )(
            conv_x,
            conv_bc,
            step,
            cum,
            upstream,
            mixed_y,
            old_states,
            conv_in,
            taps[:, :inner],
            head_rows,
            spread1,
            spread2,
            skip_row,
            conv_in,
            *sums,
            *in_place,
        )

    made = back(0, grad_y, None)
    out_own, *made = tie(out_own, *made)
    arrived = lax.ppermute(out_other, "tensor", [(i, i ^ 1) for i in range(tensor)])
    out_kept, out_leaving = zip(
        *(core_sums(out_own[:, seq], arrived[:, seq]) for seq in range(seqs))
    )
    grad_y, *flat_leaving = tie(grad_y, *sum(out_leaving, []))
    each = columns - 1
    out_leaving = [flat_leaving[i * each : (i + 1) * each] for i in range(seqs)]
    made = back(1, grad_y, made)
    arrivals = [column_sends(sent) for sent in out_leaving]
    grad_in, grad_bc_part, grad_delta, tap_fold, head_fold = back(2, grad_y, made)
    grad_in, *flat_arrivals = tie(grad_in, *sum(arrivals, []))
    arrivals = [flat_arrivals[i * each : (i + 1) * each] for i in range(seqs)]

    bc_chip = chip_total(grad_bc_part)
    in_grad = weight_grad(normed, grad_in).astype(BF)

    in_parts = lax.all_to_all(in_grad, "dp", split_axis=0, concat_axis=0, tiled=True)
    grad_delta, in_grad, bc_chip = tie(grad_delta, in_grad, bc_chip)
    bc_moved = column_total_sends(bc_chip)
    normed_own, normed_other = pl.pallas_call(
        join_kernel,
        grid=(seqs, wide_blocks),
        in_specs=[
            scalar_spec,
            by_rows(inner),
            by_rows(inner),
            by_rows(LANES),
            pl.BlockSpec((model, inner), lambda s, t: (0, 0)),
            pl.BlockSpec((model, inner), lambda s, t: (0, 0)),
            pl.BlockSpec((model, LANES), lambda s, t: (0, (inner + states) // LANES)),
        ],
        out_specs=[partial_spec, partial_spec],
        out_shape=[seen((columns, seqs, length, share), BF)] * 2,
        compiler_params=params(2),
        cost_estimate=cost(33 * 10**9, tokens_here * (2 * model + 4 * inner)),
        name="join",
    )(
        starts,
        grad_gate,
        grad_in,
        grad_delta,
        second_weight,
        first_weight,
        first_weight,
    )
    normed_other, bc_moved = tie(normed_other, bc_moved)
    normed_arrived = lax.ppermute(normed_other, "tensor", [(i, i ^ 1) for i in range(tensor)])
    bc_total = finish_total(bc_chip, bc_moved)
    out_sums = []
    for kept, moved in zip(out_kept, arrivals):
        for part in moved:
            kept = kept + part.astype(F32)
        out_sums.append(kept)
    result = (inputs_share + jnp.stack(out_sums)).astype(BF)

    grad_small, bc_tap_fold = pl.pallas_call(
        functools.partial(bc_kernel, kwidth),
        grid=(seqs,),
        in_specs=[per_seq(states), per_seq(states), fixed((8, states), 1), per_seq(LANES)],
        out_specs=[per_seq(states + LANES), fixed((8 * kwidth + 8, states), 1)],
        out_shape=[
            seen((seqs, length, states + LANES), BF),
            seen((8 * kwidth + 8, states)),
        ],
        scratch_shapes=[
            pltpu.VMEM((length + 8, states), F32),
            pltpu.VMEM((length + 8, states), F32),
        ],
        compiler_params=params(1),
        cost_estimate=cost(8 * 10**9, tokens_here * states * 12),
        name="bc_back",
    )(bc_total, bc_pre, taps[:, inner:], grad_delta)
    small_grad = weight_grad(normed, grad_small).astype(BF)
    small_parts = lax.all_to_all(small_grad, "dp", split_axis=0, concat_axis=0, tiled=True)
    small_grad, normed_own = tie(small_grad, normed_own)
    normed_kept, normed_leaving = core_sums(normed_own, normed_arrived)
    normed_moved = column_sends(normed_leaving)
    early_wide = early_share.astype(F32)
    gate_share = early_wide[:, :inner]
    out_share = early_wide[:, inner:]
    in_share = sum_parts(in_parts)
    small_share = sum_parts(small_parts)
    bc_share = small_share[:, :states]
    dt_share = small_share[:, states : states + heads]
    gate_m = momentum_rate * zx_moment[:, 0, :] + gate_share
    out_m = momentum_rate * out_moment.T + out_share
    in_m = momentum_rate * zx_moment[:, 1, :] + in_share
    bc_m = momentum_rate * bc_moment + bc_share
    dt_m = momentum_rate * dt_moment + dt_share
    early = jnp.concatenate(
        [gate_share + momentum_rate * gate_m, out_share + momentum_rate * out_m], axis=1
    )
    late = jnp.concatenate(
        [in_share + momentum_rate * in_m, bc_share + momentum_rate * bc_m], axis=1
    )
    dt_input = dt_share + momentum_rate * dt_m
    squares = jnp.sum(dt_input * dt_input, axis=0)
    units, slots = gram_units(early, late, squares)
    units, *normed_moved = tie(units, *normed_moved)
    ortho, dt_scale = orthogonal(early, late, units, slots, heads)
    bc_rows = lax.dynamic_slice(first_weight, (share_start, inner), (share, states))
    normed_share = normed_kept
    for moved in normed_moved:
        normed_share = normed_share + moved.astype(F32)
    normed_share = normed_share + jnp.einsum(
        "btk,fk->btf", grad_small[:, :, :states], bc_rows, preferred_element_type=F32
    )

    gain_share = lax.dynamic_slice_in_dim(norm_gain, share_start, share, 0)
    weighted = normed_share * gain_share
    gain_grad_share = jnp.sum(normed_share * inputs_share * inv_rms, axis=(0, 1))
    gain_padded = lax.dynamic_update_slice_in_dim(
        jnp.zeros((model,), F32), gain_grad_share, share_start, 0
    )
    inner_rows = jnp.sum(weighted * inputs_share, axis=-1)
    final_sums = tensor_sum(jnp.concatenate([inner_rows.reshape(-1), gain_padded]))
    inner_sum = final_sums[: seqs * length].reshape(seqs, length)
    gain_part = final_sums[seqs * length :]
    upstream_share = lax.dynamic_slice_in_dim(cotangent, share_start, share, 2).astype(F32)
    input_grad = (
        upstream_share
        + inv_rms * weighted
        - inputs_share * inv_rms**3 * (inner_sum / model)[..., None]
    )

    tap_sums = tap_fold.reshape(kwidth + 2, 8, inner).sum(axis=1)
    head_sums = head_fold.reshape(2, 8, LANES).sum(axis=1)[:, :heads]
    skip_grad = tap_sums[kwidth + 1].reshape(heads, head_width).sum(axis=1)
    pieces = [
        tap_sums[: kwidth + 1].reshape(-1),
        gain_fold.sum(axis=0),
        head_sums.reshape(-1),
        skip_grad,
        bc_tap_fold.reshape(kwidth + 1, 8, states).sum(axis=1).reshape(-1),
        gain_part,
    ]
    flat = dp_sum(jnp.concatenate(pieces))
    xpar_count = (kwidth + 2) * inner
    xpar_g = flat[:xpar_count].reshape(kwidth + 2, inner)
    head_g = flat[xpar_count : xpar_count + 3 * heads].reshape(3, heads)
    bcpar_g = flat[xpar_count + 3 * heads : -model].reshape(kwidth + 1, states)
    gain_g = flat[-model:]

    early_ortho = ortho[:, : 2 * inner]
    late_ortho = ortho[:, 2 * inner :]
    dt_ortho = dt_input * dt_scale
    shrink = 1.0 - matrix_rate * weight_decay
    zx_m = jnp.stack([gate_m, in_m], axis=1)
    zx_new = w_zx * shrink - matrix_rate * jnp.stack(
        [early_ortho[:, :inner], late_ortho[:, :inner]], axis=1
    )
    bc_new = state_proj_weight * shrink - matrix_rate * late_ortho[:, inner:]
    dt_new = step_weight * shrink - matrix_rate * dt_ortho
    out_new = exit_coefficient_matrix * shrink - matrix_rate * early_ortho[:, inner:].T
    gain_m = momentum_rate * gain_moment + gain_g
    xpar_m = momentum_rate * xpar_moment + xpar_g
    bcpar_m = momentum_rate * bcpar_moment + bcpar_g
    head_m = momentum_rate * head_moment + head_g
    gain_new = norm_gain - small_rate * (gain_g + momentum_rate * gain_m)
    xpar_new = x_params - small_rate * (xpar_g + momentum_rate * xpar_m)
    bcpar_new = bc_params - small_rate * (bcpar_g + momentum_rate * bcpar_m)
    head_new = head_params - small_rate * (head_g + momentum_rate * head_m)
    return (
        result,
        input_grad,
        zx_m,
        zx_new,
        bc_m,
        bc_new,
        dt_m,
        dt_new,
        out_m.T,
        out_new,
        gain_m,
        gain_new,
        xpar_m,
        xpar_new,
        bcpar_m,
        bcpar_new,
        head_m,
        head_new,
    )


def solution(mesh):
    return jax.shard_map(
        local,
        mesh=mesh,
        in_specs=(
            P("dp", None, None),
            P("dp", None, None),
            P(),
            P("dp", None, "tensor"),
            P("dp", None),
            P("dp", "tensor"),
            P("tensor", "dp"),
            P(None, "tensor"),
            P(),
            P(None, "tensor"),
            P("dp", None, "tensor"),
            P("dp", None),
            P("dp", "tensor"),
            P("tensor", "dp"),
            P(),
            P(None, "tensor"),
            P(),
            P(None, "tensor"),
        ),
        out_specs=(
            P("dp", None, "tensor"),
            P("dp", None, "tensor"),
            P("dp", None, "tensor"),
            P("dp", None, "tensor"),
            P("dp", None),
            P("dp", None),
            P("dp", "tensor"),
            P("dp", "tensor"),
            P("tensor", "dp"),
            P("tensor", "dp"),
            P(),
            P(),
            P(None, "tensor"),
            P(None, "tensor"),
            P(),
            P(),
            P(None, "tensor"),
            P(None, "tensor"),
        ),
        check_vma=False,
    )
```

```python
import functools

import jax
import jax.numpy as jnp
from jax import lax
from jax.experimental import pallas as pl
from jax.experimental.pallas import tpu as pltpu
from jax.sharding import PartitionSpec as P

BF = jnp.bfloat16
F32 = jnp.float32
CHUNK = 128
LANES = 128
ROWS = 256
PIECE = 64
WIDE_ROWS = 512
VMEM_BYTES = 52 * 1024 * 1024

exact = lax.Precision.HIGHEST
norm_eps = 1e-05
poly_first = 3.4445
poly_second = -4.775
poly_third = 2.0315
momentum_rate = 0.95
matrix_rate = 0.5
weight_decay = 0.1
small_rate = 0.0025


def params(count):
    return pltpu.CompilerParams(
        dimension_semantics=("arbitrary",) * count, vmem_limit_bytes=VMEM_BYTES
    )


def cost(flops, moved, transcendentals=0):
    return pl.CostEstimate(
        flops=flops // 40, bytes_accessed=moved // 40, transcendentals=transcendentals // 40
    )


def sigmoid(value):
    return 0.5 * jnp.tanh(0.5 * value) + 0.5


def dot(left, right):
    return jnp.dot(left, right, preferred_element_type=F32)


def dot_nt(left, right):
    return lax.dot_general(left, right, (((1,), (1,)), ((), ())), preferred_element_type=F32)


def halves(value):
    high = value.astype(BF)
    low = (value - high.astype(F32)).astype(BF)
    return high, low


def spread_dot(value, spread):
    high, low = halves(value)
    return dot(jnp.concatenate([high, low], axis=1), spread)


def gather_dot(value, spread):
    high, low = halves(value)
    return dot_nt(high, spread) + dot_nt(low, spread)


def tri_dot(triangle, value):
    first = value.astype(BF)
    rest = value - first.astype(F32)
    second = rest.astype(BF)
    third = (rest - second.astype(F32)).astype(BF)
    return dot(triangle, first) + dot(triangle, second) + dot(triangle, third)


def flip(value):
    return value.astype(F32).T.astype(BF)


def row_fold(value):
    return value.reshape(-1, 8, value.shape[-1]).sum(axis=0)


def tiles_of(start, stop, step):
    return [(low, min(step, stop - low)) for low in range(start, stop, step)]


def iota(shape, axis):
    return lax.broadcasted_iota(jnp.int32, shape, axis)


def project_kernel(
    kwidth, normed, weight, taps, heads, conv_in, bc_pre, conv_x, conv_bc, step, cum, buffer
):
    inner = conv_in.shape[-1]
    states = bc_pre.shape[-1]
    rows = normed.shape[1]
    block = pl.program_id(1)

    @pl.when(block == 0)
    def _():
        buffer[0:8, :] = jnp.zeros((8, inner + states), F32)

    @pl.when(block > 0)
    def _():
        buffer[0:8, :] = buffer[rows : rows + 8, :]

    data = normed[0]
    for low, width in tiles_of(0, inner, 256) + tiles_of(inner, inner + states, 256):
        cols = slice(low, low + width)
        made = dot(data, weight[:, cols])
        buffer[8 : 8 + rows, cols] = made
        for top in range(0, rows, PIECE):
            for left in range(low, low + width, LANES):
                here = slice(left, left + LANES)
                kept = buffer[8 + top : 8 + top + PIECE, here]
                total = taps[kwidth : kwidth + 1, here] + taps[kwidth - 1 : kwidth, here] * kept
                for offset in range(kwidth - 1):
                    start = 9 - kwidth + offset + top
                    total = total + taps[offset : offset + 1, here] * (
                        buffer[start : start + PIECE, here]
                    )
                active = (total * sigmoid(total)).astype(BF)
                span = slice(top, top + PIECE)
                if left < inner:
                    conv_in[0, span, here] = kept.astype(BF)
                    conv_x[0, span, here] = active
                else:
                    own = slice(left - inner, left - inner + LANES)
                    bc_pre[0, span, own] = kept
                    conv_bc[0, span, own] = active
    delta = dot(data, weight[:, inner + states :]) + heads[1:2, :]
    size = jnp.maximum(delta, 0.0) + jnp.log1p(jnp.exp(-jnp.abs(delta)))
    decay = -size * jnp.exp(heads[0:1, :])
    step[0] = size
    lower = (iota((CHUNK, CHUNK), 0) >= iota((CHUNK, CHUNK), 1)).astype(F32).astype(BF)
    for low in range(0, rows, CHUNK):
        cum[0, low : low + CHUNK, :] = tri_dot(lower, decay[low : low + CHUNK, :])


def scan_kernel(conv_x, conv_bc, step, cum, spread2, skip, y, states, state):
    inner = conv_x.shape[-1]
    width = conv_bc.shape[-1] // 2
    state[...] = jnp.zeros_like(state)
    causal = iota((CHUNK, CHUNK), 0) >= iota((CHUNK, CHUNK), 1)
    first = iota((CHUNK, LANES), 1) < LANES // 2
    spread = spread2[...]

    def body(index, carry):
        rows = pl.ds(pl.multiple_of(index * CHUNK, CHUNK), CHUNK)
        value = conv_x[0, rows, :]
        b_part = conv_bc[0, rows, :width]
        c_part = conv_bc[0, rows, width:]
        running = cum[0, rows, :]
        size = step[0, rows, :]
        state_low = state[...].astype(BF)
        states[0, index] = state_low
        scores = dot_nt(c_part, b_part)
        carried = dot(c_part, state_low)
        grow = spread_dot(jnp.exp(running), spread)
        tail = spread_dot(size * jnp.exp(running[CHUNK - 1 : CHUNK, :] - running), spread)
        keys = (running - jnp.log(size)).T
        for pair in range(inner // LANES):
            cols = slice(pair * LANES, (pair + 1) * LANES)
            pair_x = value[:, cols]
            stacked = []
            for head in (2 * pair, 2 * pair + 1):
                gap = running[:, head : head + 1] - keys[head : head + 1, :]
                stacked.append(jnp.where(causal, jnp.exp(gap) * scores, 0.0).astype(BF))
            parts = dot(jnp.concatenate(stacked, axis=0), pair_x)
            y[0, rows, cols] = (
                jnp.where(first, parts[:CHUNK], parts[CHUNK:])
                + carried[:, cols] * grow[:, cols]
                + skip[0:1, cols] * pair_x.astype(F32)
            )
        weighted = (value.astype(F32) * tail).astype(BF)
        state[...] = state[...] * grow[CHUNK - 1 : CHUNK, :] + dot(flip(b_part), weighted)
        return carry

    lax.fori_loop(0, conv_x.shape[1] // CHUNK, body, 0)


def gate_kernel(normed, cotangent, weight, y, gain, gate_pre, grad_mixed, stats):
    inner = y.shape[-1]
    rows = normed.shape[1]
    data = normed[0]
    upstream = cotangent[0]
    squares = [jnp.zeros((PIECE, LANES), F32) for _ in range(rows // PIECE)]
    products = [jnp.zeros((PIECE, LANES), F32) for _ in range(rows // PIECE)]
    for low, width in tiles_of(0, inner, 256):
        cols = slice(low, low + width)
        pre_all = dot(data, weight[:, cols])
        grad_all = dot(upstream, weight[:, inner + low : inner + low + width])
        gate_pre[0, :, cols] = pre_all.astype(BF)
        grad_mixed[0, :, cols] = grad_all.astype(BF)
        for piece in range(rows // PIECE):
            span = slice(piece * PIECE, (piece + 1) * PIECE)
            for left in range(0, width, LANES):
                here = slice(low + left, low + left + LANES)
                pre = pre_all[span, left : left + LANES]
                gated = y[0, span, here] * pre * sigmoid(pre)
                squares[piece] = squares[piece] + gated * gated
                products[piece] = products[piece] + (
                    grad_all[span, left : left + LANES] * gain[0:1, here] * gated
                )
    squares = jnp.concatenate(squares, axis=0)
    products = jnp.concatenate(products, axis=0)
    lane = iota((rows, LANES), 1)
    both = jnp.where(
        lane == 0,
        jnp.sum(squares, axis=1, keepdims=True),
        jnp.where(lane == 1, jnp.sum(products, axis=1, keepdims=True), 0.0),
    )
    stats[0] = both.T[0:8, :]


def mix_kernel(
    starts,
    y,
    gate_pre,
    grad_mixed,
    scales,
    gain,
    weight,
    mixed,
    grad_y,
    grad_gate,
    own_core,
    other_core,
    gain_sum,
):
    inner = y.shape[-1]
    rows = y.shape[1]

    @pl.when((pl.program_id(0) == 0) & (pl.program_id(1) == 0))
    def _():
        gain_sum[...] = jnp.zeros_like(gain_sum)

    by_row = scales[0].T
    inverse = by_row[:, 0:1]
    slope = by_row[:, 1:2]
    for low in range(0, inner, LANES):
        cols = slice(low, low + LANES)
        gain_here = gain[0:1, cols]
        folded = jnp.zeros((8, LANES), F32)
        for top in range(0, rows, PIECE):
            span = slice(top, top + PIECE)
            value = y[0, span, cols]
            pre = gate_pre[0, span, cols].astype(F32)
            upstream = grad_mixed[0, span, cols].astype(F32)
            logistic = sigmoid(pre)
            act = pre * logistic
            gated = value * act
            scaled = gated * inverse[span]
            folded = folded + row_fold(upstream * scaled)
            mixed[0, span, cols] = (scaled * gain_here).astype(BF)
            grad_gated = inverse[span] * (upstream * gain_here) - gated * slope[span]
            grad_y[0, span, cols] = (grad_gated * act).astype(BF)
            grad_gate[0, span, cols] = (
                grad_gated * value * (logistic * (1.0 + pre * (1.0 - logistic)))
            ).astype(BF)
        gain_sum[:, cols] += folded
    data = mixed[0]
    share = own_core.shape[-1]
    columns = own_core.shape[0]
    for part in range(2 * columns):
        rows = pl.ds(pl.multiple_of(starts[part], share), share)
        made = dot_nt(data, weight[rows, :]).astype(BF)
        if part < columns:
            own_core[part, 0] = made
        else:
            other_core[part - columns, 0] = made


def back_kernel(
    kwidth,
    conv_x,
    conv_bc,
    step,
    cum,
    grad_y,
    y,
    states,
    conv_in,
    taps,
    heads,
    spread1,
    spread2,
    skip,
    in_before,
    old_taps,
    old_heads,
    after_in,
    after_bc,
    after_delta,
    grad_in,
    grad_bc,
    grad_delta,
    tap_sums,
    head_sums,
    grad_state,
    back_buffer,
    in_buffer,
):
    inner = conv_x.shape[-1]
    width = conv_bc.shape[-1] // 2
    chunks = conv_x.shape[1] // CHUNK
    step_index = pl.program_id(0)
    first_block = step_index == pl.num_programs(0) - 1

    @pl.when(step_index == 0)
    def _():
        tap_sums[...] = old_taps[...]
        head_sums[...] = old_heads[...]
        grad_state[...] = jnp.zeros_like(grad_state)
        back_buffer[0:8, :] = jnp.zeros((8, inner), F32)

    anti = iota((CHUNK, CHUNK), 0) <= iota((CHUNK, CHUNK), 1)
    upper = anti.astype(F32).astype(BF)
    first = iota((CHUNK, LANES), 1) < LANES // 2
    rate = jnp.exp(heads[0:1, :])
    spread = spread2[...]
    gather = spread1[...]

    for index in reversed(range(chunks)):
        rows = slice(index * CHUNK, (index + 1) * CHUNK)
        value = conv_x[0, rows, :]
        b_part = conv_bc[0, rows, :width]
        c_part = conv_bc[0, rows, width:]
        running = cum[0, rows, :]
        size = step[0, rows, :]
        upstream = grad_y[0, rows, :]
        old_state = states[0, index]
        state_grad = grad_state[...]
        state_grad_low = state_grad.astype(BF)
        scores = dot_nt(b_part, c_part)
        reach = dot(b_part, state_grad_low)
        grow = spread_dot(jnp.exp(running), spread)
        tail = spread_dot(size * jnp.exp(running[CHUNK - 1 : CHUNK, :] - running), spread)
        grown = (upstream.astype(F32) * grow).astype(BF)
        weighted = (value.astype(F32) * tail).astype(BF)
        grad_c = dot_nt(grown, old_state)
        grad_b = dot_nt(weighted, state_grad_low)
        last_grow = grow[CHUNK - 1 : CHUNK, :]
        grad_state[...] = state_grad * last_grow + dot(flip(c_part), grown)
        kept = row_fold(old_state.astype(F32) * state_grad) * last_grow
        queries = running.T
        keys = running - jnp.log(size)
        score_grad = jnp.zeros((CHUNK, CHUNK), F32)
        flow_parts = []
        pull_parts = []
        end_parts = []
        if index > 0:
            in_buffer[0:16, :] = conv_in[0, index * CHUNK - 16 : index * CHUNK, :].astype(F32)
        else:
            in_buffer[0:16, :] = jnp.where(first_block, 0.0, in_before[0].astype(F32))
        in_buffer[16 : 16 + CHUNK, :] = conv_in[0, rows, :].astype(F32)
        back_buffer[CHUNK : CHUNK + 8, :] = back_buffer[0:8, :]
        for pair in range(inner // LANES):
            cols = slice(pair * LANES, (pair + 1) * LANES)
            pair_x = value[:, cols]
            pair_up = upstream[:, cols]
            kernels = []
            for head in (2 * pair, 2 * pair + 1):
                gap = queries[head : head + 1, :] - keys[:, head : head + 1]
                kernels.append(jnp.where(anti, jnp.exp(gap), 0.0))
            nothing = jnp.zeros_like(pair_x)
            own_x = jnp.concatenate(
                [jnp.where(first, pair_x, nothing), jnp.where(first, nothing, pair_x)], axis=0
            )
            products = dot_nt(own_x, pair_up)
            score_grad = (
                score_grad + kernels[0] * products[:CHUNK] + kernels[1] * products[CHUNK:]
            )
            stacked = [(kernel * scores).astype(BF) for kernel in kernels]
            parts = dot(jnp.concatenate(stacked, axis=0), pair_up)
            x_wide = pair_x.astype(F32)
            up_wide = pair_up.astype(F32)
            far = reach[:, cols] * tail[:, cols]
            inside = jnp.where(first, parts[:CHUNK], parts[CHUNK:]) + far
            skip_row = skip[0:1, cols]
            pull = x_wide * inside
            pull_parts.append(pull)
            flow_parts.append(up_wide * (y[0, rows, cols] - skip_row * x_wide) - pull)
            end_parts.append(row_fold(x_wide * far) + kept[:, cols])
            grad_x = inside + skip_row * up_wide
            now = in_buffer[16 : 16 + CHUNK, cols]
            shifted = [
                in_buffer[17 - kwidth + offset : 17 - kwidth + offset + CHUNK, cols]
                for offset in range(kwidth - 1)
            ] + [now]
            total = taps[kwidth : kwidth + 1, cols]
            for offset in range(kwidth):
                total = total + taps[offset : offset + 1, cols] * shifted[offset]
            logistic = sigmoid(total)
            error = grad_x * (logistic * (1.0 + total * (1.0 - logistic)))
            back_buffer[0:CHUNK, cols] = error
            for offset in range(kwidth):
                tap_sums[8 * offset : 8 * offset + 8, cols] += row_fold(error * shifted[offset])
            tap_sums[8 * kwidth : 8 * kwidth + 8, cols] += row_fold(error)
            tap_sums[8 * kwidth + 8 : 8 * kwidth + 16, cols] += row_fold(x_wide * up_wide)
            moved = taps[kwidth - 1 : kwidth, cols] * error
            for offset in range(kwidth - 1):
                start = kwidth - 1 - offset
                moved = moved + (
                    taps[offset : offset + 1, cols] * back_buffer[start : start + CHUNK, cols]
                )
            grad_in[0, rows, cols] = moved.astype(BF)
        score_low = score_grad.astype(BF)
        grad_bc[0, rows, :width] = (grad_b + dot(score_low, c_part)).astype(BF)
        grad_bc[0, rows, width:] = (grad_c + dot(flip(score_grad), b_part)).astype(BF)
        flow = gather_dot(jnp.concatenate(flow_parts, axis=1), gather)
        pull = gather_dot(jnp.concatenate(pull_parts, axis=1), gather)
        ends = gather_dot(jnp.concatenate(end_parts, axis=1), gather)
        decay_grad = tri_dot(upper, flow) + jnp.sum(ends, axis=0, keepdims=True)
        size_grad = pull / jnp.maximum(size, 1e-37) - rate * decay_grad
        small = size * (1.0 - size * (0.5 - size * (1.0 / 6.0)))
        delta_grad = size_grad * jnp.where(size < 0.01, small, 1.0 - jnp.exp(-size))
        grad_delta[0, rows, :] = delta_grad.astype(BF)
        head_sums[0:8, :] += row_fold(decay_grad * (-size * rate))
        head_sums[8:16, :] += row_fold(delta_grad)


def join_kernel(
    starts, grad_gate, grad_in, grad_delta, gate_weight, in_weight, step_weight, own_core, other_core
):
    share = own_core.shape[-1]
    columns = own_core.shape[0]
    for part in range(2 * columns):
        rows = pl.ds(pl.multiple_of(starts[part], share), share)
        total = dot_nt(grad_gate[0], gate_weight[rows, :])
        total = total + dot_nt(grad_in[0], in_weight[rows, :])
        total = total + dot_nt(grad_delta[0], step_weight[rows, :])
        if part < columns:
            own_core[part, 0] = total.astype(BF)
        else:
            other_core[part - columns, 0] = total.astype(BF)


def bc_kernel(kwidth, summed, pre, taps, grad_delta, grad_small, tap_sums, before, later):
    length = pre.shape[1]
    width = pre.shape[2]

    @pl.when(pl.program_id(0) == 0)
    def _():
        tap_sums[...] = jnp.zeros_like(tap_sums)

    before[0:8, :] = jnp.zeros((8, width), F32)
    before[8 : 8 + length, :] = pre[0]
    later[length : length + 8, :] = jnp.zeros((8, width), F32)
    for left in range(0, width, LANES):
        here = slice(left, left + LANES)

        folds = [jnp.zeros((8, LANES), F32) for _ in range(kwidth + 1)]
        for top in range(0, length, PIECE):
            span = slice(top, top + PIECE)
            shifted = [
                before[top + 9 - kwidth + offset : top + 9 - kwidth + offset + PIECE, here]
                for offset in range(kwidth)
            ]
            total = taps[kwidth : kwidth + 1, here]
            for offset in range(kwidth):
                total = total + taps[offset : offset + 1, here] * shifted[offset]
            logistic = sigmoid(total)
            error = summed[0, span, here].astype(F32) * (
                logistic * (1.0 + total * (1.0 - logistic))
            )
            later[span, here] = error
            for offset in range(kwidth):
                folds[offset] = folds[offset] + row_fold(error * shifted[offset])
            folds[kwidth] = folds[kwidth] + row_fold(error)
        for offset in range(kwidth + 1):
            tap_sums[8 * offset : 8 * offset + 8, here] += folds[offset]
        for top in range(0, length, PIECE):
            moved = taps[kwidth - 1 : kwidth, here] * later[top : top + PIECE, here]
            for offset in range(kwidth - 1):
                start = top + kwidth - 1 - offset
                moved = moved + taps[offset : offset + 1, here] * later[start : start + PIECE, here]
            grad_small[0, top : top + PIECE, here] = moved.astype(BF)
    grad_small[0, :, width:] = grad_delta[0]


def block_mask():
    half = LANES // 2
    return (iota((LANES, LANES), 0) < half) == (iota((LANES, LANES), 1) < half)


def pair_pack(matrix):
    half = LANES // 2
    return jnp.where(iota((half, LANES), 1) < half, matrix[:half], matrix[half:])


def pair_unpack(unit):
    half = LANES // 2
    left = iota((half, LANES), 1) < half
    return jnp.concatenate([jnp.where(left, unit, 0.0), jnp.where(left, 0.0, unit)], axis=0)


def gram_kernel(slots, first, second, squares, units):
    half = LANES // 2
    pairs, wholes, single = slots
    units[...] = jnp.zeros_like(units)
    split = first.shape[1] // LANES
    for index in range(pairs + len(wholes)):
        source, at = (first, index) if index < split else (second, index - split)
        part = source[:, at * LANES : (at + 1) * LANES]
        made = jnp.dot(part.T, part, precision=exact, preferred_element_type=F32)
        if index < pairs:
            units[index] = pair_pack(made)
        else:
            slot = wholes[index - pairs]
            units[slot] = made[:half]
            units[slot + 1] = made[half:]
    units[single, 0:8, :] = squares[...]


def newton_kernel(parts, kinds, result):
    half = LANES // 2
    same = block_mask()
    eye = (iota((LANES, LANES), 0) == iota((LANES, LANES), 1)).astype(F32)
    low_row = iota((LANES, 1), 0) < half
    low_col = iota((1, LANES), 1) < half

    def mul(left, right):
        return jnp.dot(left, right, precision=exact, preferred_element_type=F32)

    count = result.shape[0]
    sums = []
    for index in range(count):
        total = parts[0, index]
        for source in range(1, parts.shape[0]):
            total = total + parts[source, index]
        sums.append(total)
    whole = kinds[0:1, :] > 0.5
    is_whole = whole[:, 0:1]
    grams = [pair_unpack(unit) for unit in sums]
    grams[0] = jnp.where(whole, jnp.concatenate(sums[:2], axis=0), grams[0])
    scales = []
    for index in range(count):
        diagonal = jnp.sum(grams[index] * eye, axis=0, keepdims=True)
        low_trace = jnp.sum(jnp.where(low_col, diagonal, 0.0), axis=1, keepdims=True)
        high_trace = jnp.sum(jnp.where(low_col, 0.0, diagonal), axis=1, keepdims=True)
        if index == 0:
            both = low_trace + high_trace
            low_trace = jnp.where(is_whole, both, low_trace)
            high_trace = jnp.where(is_whole, both, high_trace)
        low_scale = 1.0 / (jnp.sqrt(low_trace) + 1e-07)
        high_scale = 1.0 / (jnp.sqrt(high_trace) + 1e-07)
        scale_row = jnp.where(low_row, low_scale, high_scale)
        scale_col = jnp.where(low_col, low_scale, high_scale)
        grams[index] = grams[index] * scale_row * scale_col
        scales.append(scale_row)
    totals = [None] * count
    for sweep in range(5):
        squares = [mul(gram, gram) for gram in grams]
        factors = [
            poly_first * eye + poly_second * gram + poly_third * square
            for gram, square in zip(grams, squares)
        ]
        totals = [
            scale * factor if sweep == 0 else mul(total, factor)
            for scale, total, factor in zip(scales, totals, factors)
        ]
        if sweep < 4:
            halfway = [mul(factor, gram) for factor, gram in zip(factors, grams)]
            grams = [mul(left, factor) for left, factor in zip(halfway, factors)]
    for index in range(count):
        made = pair_pack(totals[index])
        if index < 2:
            here = totals[0][:half] if index == 0 else totals[0][half:]
            made = jnp.where(whole, here, made)
        length = sums[index]
        scale = 1.0 / (jnp.sqrt(length) + 1e-07)
        length = length * scale * scale
        for sweep in range(5):
            step = poly_first + length * (poly_second + poly_third * length)
            scale = scale * step
            length = length * step * step
        single = kinds[8 + index : 9 + index, :] > 0.5
        result[index] = jnp.where(single, scale, made).astype(BF)


def apply_kernel(slots, first, second, units, made):
    pairs, wholes, single = slots
    split = first.shape[1] // LANES
    for index in range(pairs + len(wholes)):
        source, at = (first, index) if index < split else (second, index - split)
        if index < pairs:
            factor = pair_unpack(units[index].astype(F32))
        else:
            slot = wholes[index - pairs]
            factor = jnp.concatenate([units[slot], units[slot + 1]], axis=0).astype(F32)
        made[:, index * LANES : (index + 1) * LANES] = jnp.dot(
            source[:, at * LANES : (at + 1) * LANES],
            factor,
            precision=exact,
            preferred_element_type=F32,
        )


def whole_call(kernel, shapes, *operands):
    return pl.pallas_call(
        kernel,
        out_shape=shapes,
        compiler_params=pltpu.CompilerParams(vmem_limit_bytes=VMEM_BYTES),
    )(*operands)


def seen(shape, dtype=F32):
    return jax.ShapeDtypeStruct(shape, dtype)


def by_rows(width, rows=WIDE_ROWS):
    return pl.BlockSpec((1, rows, width), lambda s, t: (s, t, 0))


def fixed(shape, count):
    if count == 2:
        return pl.BlockSpec(shape, lambda s, t: (0,) * len(shape))
    return pl.BlockSpec(shape, lambda s: (0,) * len(shape))


def pad_rows(array, rows=8):
    return jnp.pad(array, ((0, rows - array.shape[0]), (0, 0)))


def pad_cols(array, cols):
    return jnp.pad(array, ((0, 0), (0, cols - array.shape[1])))


def copy_to_all(array, axis):
    count = lax.axis_size(axis)
    return lax.all_to_all(
        jnp.broadcast_to(array, (count,) + array.shape), axis, split_axis=0, concat_axis=0, tiled=True
    )


def block_starts(share):
    columns = lax.axis_size("tensor") // 2
    me = lax.axis_index("tensor")
    order = (me // 2 + jnp.arange(columns)) % columns
    return (
        share * jnp.concatenate([2 * order + me % 2, 2 * order + 1 - me % 2])
    ).astype(jnp.int32)


def core_sums(own, arrived):
    kept = own[0].astype(F32) + arrived[0].astype(F32)
    leaving = [
        (own[shift].astype(F32) + arrived[shift].astype(F32)).astype(BF)
        for shift in range(1, own.shape[0])
    ]
    return kept, leaving


def core_phase(own, other):
    count = lax.axis_size("tensor")
    return core_sums(own, lax.ppermute(other, "tensor", [(i, i ^ 1) for i in range(count)]))


def column_sends(leaving):
    count = lax.axis_size("tensor")
    columns = count // 2
    return [
        lax.ppermute(
            sent,
            "tensor",
            [(i, ((i // 2 + shift) % columns) * 2 + i % 2) for i in range(count)],
        )
        for shift, sent in enumerate(leaving, 1)
    ]


def column_phase(kept, leaving):
    for moved in column_sends(leaving):
        kept = kept + moved.astype(F32)
    return kept


def tensor_sum(value):
    count = lax.axis_size("tensor")
    step = 1
    while step < count:
        value = value + lax.ppermute(value, "tensor", [(i, i ^ step) for i in range(count)])
        step *= 2
    return value


def after(value, *others):
    return lax.optimization_barrier((value,) + others)[0]


def tie(*values):
    return lax.optimization_barrier(values)


def gather_rows(shard):
    count = lax.axis_size("dp")
    if count != 8:
        return lax.all_gather(shard, "dp", axis=0, tiled=True), shard, shard
    rows = shard.shape[0]
    me = lax.axis_index("dp")
    z = me // 2
    y = me % 2
    result = jnp.zeros((9 * rows, shard.shape[1]), shard.dtype)
    swap = [(i, i ^ 1) for i in range(count)]

    def place(result, piece, z_from, y_from):
        there = (z_from >= 0) & (z_from < 4)
        start = jnp.where(there, (z_from * 2 + y_from) * rows, 8 * rows)
        return lax.dynamic_update_slice_in_dim(result, piece, start, 0)

    other = lax.ppermute(shard, "dp", swap)
    result = place(result, shard, z, y)
    up = down = shard
    for step in range(1, 4):
        up = lax.ppermute(
            up, "dp", [(2 * i + j, 2 * i + 2 + j) for i in range(step - 1, 3) for j in range(2)]
        )
        down = lax.ppermute(
            down, "dp", [(2 * i + j, 2 * i - 2 + j) for i in range(1, 5 - step) for j in range(2)]
        )
        if step == 1:
            up, down, other = tie(up, down, other)
        result = place(place(result, up, z - step, y), down, z + step, y)
    leaving = jnp.concatenate(
        [
            lax.dynamic_slice_in_dim(result, ((z ^ k) * 2 + y) * rows, rows, 0)
            for k in range(1, 4)
        ],
        axis=0,
    )
    arrived = lax.ppermute(leaving, "dp", swap)
    result = place(result, other, z, 1 - y)
    for k in range(1, 4):
        result = place(result, arrived[(k - 1) * rows : k * rows], z ^ k, 1 - y)
    return result, up, down


def sum_parts(parts):
    count = lax.axis_size("dp")
    return parts.reshape(count, -1, parts.shape[1]).astype(F32).sum(axis=0)


def add_low(left, right):
    return (left.astype(F32) + right.astype(F32)).astype(BF)


def chip_total(value):
    count = lax.axis_size("tensor")
    half = value.shape[1] // 2
    arrived = lax.ppermute(value, "tensor", [(i, i ^ 1) for i in range(count)])
    start = lax.axis_index("tensor") % 2 * half
    return add_low(
        lax.dynamic_slice_in_dim(value, start, half, 1),
        lax.dynamic_slice_in_dim(arrived, start, half, 1),
    )


def column_total_sends(part):
    count = lax.axis_size("tensor")
    return lax.ppermute(part, "tensor", [(i, i ^ 2) for i in range(count)])


def finish_total(part, moved):
    count = lax.axis_size("tensor")
    part = add_low(part, moved)
    step = 4
    while step < count:
        part = add_low(part, lax.ppermute(part, "tensor", [(i, i ^ step) for i in range(count)]))
        step *= 2
    other = lax.ppermute(part, "tensor", [(i, i ^ 1) for i in range(count)])
    first = lax.axis_index("tensor") % 2 == 0
    return jnp.concatenate(
        [jnp.where(first, part, other), jnp.where(first, other, part)], axis=1
    )


def dp_sum(value):
    count = lax.axis_size("dp")
    step = 1
    while step < count:
        value = value + lax.ppermute(value, "dp", [(i, i ^ step) for i in range(count)])
        step *= 2
    return value


def gram_units(first, second, squares):
    dp = lax.axis_size("dp")
    half = LANES // 2
    pairs = (first.shape[1] + second.shape[1]) // LANES - 2
    each = max(2, -(-pairs // (dp - 2)))
    wholes = ((dp - 2) * each, (dp - 1) * each)
    single = wholes[0] + 2 if each > 2 else wholes[0] - each
    slots = (pairs, wholes, single)
    square_rows = pad_rows(pad_cols(squares[None], LANES))
    units = whole_call(
        functools.partial(gram_kernel, slots),
        seen((dp * each, half, LANES)),
        first,
        second,
        square_rows,
    )
    return units, slots


def newton(units, slots):
    dp = lax.axis_size("dp")
    half = LANES // 2
    each = units.shape[0] // dp
    single = slots[2]
    parts = lax.all_to_all(units, "dp", split_axis=0, concat_axis=0, tiled=True)
    me = lax.axis_index("dp")
    kinds = jnp.concatenate(
        [
            jnp.broadcast_to((me >= dp - 2).astype(F32), (8, LANES)),
            jnp.broadcast_to(
                (me * each + jnp.arange(8) == single).astype(F32)[:, None], (8, LANES)
            ),
        ],
        axis=0,
    )
    factors = whole_call(
        newton_kernel, seen((each, half, LANES), BF), parts.reshape(dp, each, half, LANES), kinds
    )
    return factors


def updates(first, second, factors, slots, count):
    dp = lax.axis_size("dp")
    half = LANES // 2
    each = factors.shape[0]
    single = slots[2]
    factors = copy_to_all(factors, "dp").reshape(dp * each, half, LANES)
    made = whole_call(
        functools.partial(apply_kernel, slots),
        seen((first.shape[0], first.shape[1] + second.shape[1])),
        first,
        second,
        factors,
    )
    return made, factors[single, 0, :count].astype(F32)


def local(
    tokens,
    cotangent,
    norm_gain,
    w_zx,
    state_proj_weight,
    step_weight,
    exit_coefficient_matrix,
    x_params,
    bc_params,
    head_params,
    zx_moment,
    bc_moment,
    dt_moment,
    out_moment,
    gain_moment,
    xpar_moment,
    bcpar_moment,
    head_moment,
):
    kwidth = bc_params.shape[0] - 1
    heads = head_params.shape[1]
    inner = x_params.shape[1]
    head_width = inner // heads
    states = bc_params.shape[1]
    seqs, length, model = tokens.shape
    tensor = lax.axis_size("tensor")
    tensor_index = lax.axis_index("tensor")
    share = model // tensor
    share_start = tensor_index * share
    whole_inner = inner * tensor
    blocks = length // ROWS
    wide_blocks = length // WIDE_ROWS
    chunks = length // CHUNK
    tokens_here = seqs * length

    first_weight, last_up, last_down = gather_rows(
        jnp.concatenate(
            [w_zx[:, 1, :], state_proj_weight, pad_cols(step_weight, LANES)], axis=1
        ).astype(BF)
    )
    second_part = jnp.concatenate([w_zx[:, 0, :], exit_coefficient_matrix.T], axis=1).astype(BF)
    second_weight = lax.all_gather(
        after(second_part, last_up, last_down), "dp", axis=0, tiled=True
    )
    wide = after(tokens, last_up, last_down, second_part).astype(F32)
    inv_rms = lax.rsqrt(jnp.mean(wide * wide, axis=-1, keepdims=True) + norm_eps)
    normed = lax.optimization_barrier((wide * inv_rms * norm_gain).astype(BF))
    any_spec = pl.BlockSpec(memory_space=pl.ANY)

    starts = block_starts(share)

    taps = pad_rows(jnp.concatenate([x_params[: kwidth + 1], bc_params], axis=1))
    head_rows = pad_rows(pad_cols(head_params, LANES))
    lane_head = jnp.arange(inner) // head_width
    spread1 = (jnp.arange(LANES)[:, None] == lane_head[None, :]).astype(BF)
    spread2 = jnp.concatenate([spread1, spread1], axis=0)
    skip_row = jnp.broadcast_to(jnp.repeat(head_params[2], head_width)[None], (8, inner))
    gain_row = jnp.broadcast_to(x_params[kwidth + 1][None], (8, inner))

    first_cols = first_weight.shape[1]
    conv_in, bc_pre, conv_x, conv_bc, step, cum = pl.pallas_call(
        functools.partial(project_kernel, kwidth),
        grid=(seqs, wide_blocks),
        in_specs=[
            by_rows(model),
            fixed((model, first_cols), 2),
            fixed((8, inner + states), 2),
            fixed((8, LANES), 2),
        ],
        out_specs=[
            by_rows(inner),
            by_rows(states),
            by_rows(inner),
            by_rows(states),
            by_rows(LANES),
            by_rows(LANES),
        ],
        out_shape=[
            seen((seqs, length, inner), BF),
            seen((seqs, length, states)),
            seen((seqs, length, inner), BF),
            seen((seqs, length, states), BF),
            seen((seqs, length, LANES)),
            seen((seqs, length, LANES)),
        ],
        scratch_shapes=[pltpu.VMEM((WIDE_ROWS + 8, inner + states), F32)],
        compiler_params=params(2),
        cost_estimate=cost(
            28 * 10**9, tokens_here * (model + 3 * inner) * 2
        ),
        name="project",
    )(normed, first_weight, taps, head_rows)

    def per_seq(width):
        return pl.BlockSpec((1, length, width), lambda s: (s, 0, 0))

    state_spec = pl.BlockSpec((1, chunks, states // 2, inner), lambda s: (s, 0, 0, 0))
    mixed_y, old_states = pl.pallas_call(
        scan_kernel,
        grid=(seqs,),
        in_specs=[
            per_seq(inner),
            per_seq(states),
            per_seq(LANES),
            per_seq(LANES),
            fixed((2 * LANES, inner), 1),
            fixed((8, inner), 1),
        ],
        out_specs=[per_seq(inner), state_spec],
        out_shape=[
            seen((seqs, length, inner)),
            seen((seqs, chunks, states // 2, inner), BF),
        ],
        scratch_shapes=[pltpu.VMEM((states // 2, inner), F32)],
        compiler_params=params(1),
        cost_estimate=cost(
            20 * 10**9, tokens_here * inner * 8, tokens_here * heads * CHUNK
        ),
        name="scan",
    )(conv_x, conv_bc, step, cum, spread2, skip_row)

    stats_spec = pl.BlockSpec((1, 8, WIDE_ROWS), lambda s, t: (s, 0, t))
    gate_pre, grad_mixed, stats = pl.pallas_call(
        gate_kernel,
        grid=(seqs, wide_blocks),
        in_specs=[
            by_rows(model),
            by_rows(model),
            fixed((model, 2 * inner), 2),
            by_rows(inner),
            fixed((8, inner), 2),
        ],
        out_specs=[by_rows(inner), by_rows(inner), stats_spec],
        out_shape=[
            seen((seqs, length, inner), BF),
            seen((seqs, length, inner), BF),
            seen((seqs, 8, length)),
        ],
        compiler_params=params(2),
        cost_estimate=cost(27 * 10**9, tokens_here * (4 * model + 8 * inner)),
        name="gate",
    )(normed, cotangent, second_weight, mixed_y, gain_row)

    sums = tensor_sum(stats[:, :2])
    inverse = lax.rsqrt(sums[:, 0] / whole_inner + norm_eps)
    slope = inverse**3 * (sums[:, 1] / whole_inner)
    scales = jnp.pad(jnp.stack([inverse, slope], axis=1), ((0, 0), (0, 6), (0, 0)))

    columns = tensor // 2
    partial_spec = pl.BlockSpec((columns, 1, WIDE_ROWS, share), lambda s, t: (0, s, t, 0))
    scalar_spec = pl.BlockSpec(memory_space=pltpu.SMEM)
    blended, grad_y, grad_gate, out_own, out_other, gain_fold = pl.pallas_call(
        mix_kernel,
        grid=(seqs, wide_blocks),
        in_specs=[
            scalar_spec,
            by_rows(inner),
            by_rows(inner),
            by_rows(inner),
            stats_spec,
            fixed((8, inner), 2),
            pl.BlockSpec((model, inner), lambda s, t: (0, 1)),
        ],
        out_specs=[
            by_rows(inner),
            by_rows(inner),
            by_rows(inner),
            partial_spec,
            partial_spec,
            fixed((8, inner), 2),
        ],
        out_shape=[
            seen((seqs, length, inner), BF),
            seen((seqs, length, inner), BF),
            seen((seqs, length, inner), BF),
            seen((columns, seqs, length, share), BF),
            seen((columns, seqs, length, share), BF),
            seen((8, inner)),
        ],
        compiler_params=params(2),
        cost_estimate=cost(
            28 * 10**9, tokens_here * (2 * model + 14 * inner)
        ),
        name="mix",
    )(starts, mixed_y, gate_pre, grad_mixed, scales, gain_row, second_weight)

    inputs_share = lax.dynamic_slice_in_dim(tokens, share_start, share, 2).astype(F32)

    def weight_grad(left, right):
        return jnp.einsum("std,stu->du", left, right, preferred_element_type=F32)

    out_grad = weight_grad(cotangent, blended).astype(BF)
    grad_gate, out_grad = tie(grad_gate, out_grad)
    gate_grad = weight_grad(normed, grad_gate).astype(BF)
    early_grad = jnp.concatenate([gate_grad, out_grad], axis=1)
    grad_y, early_grad = tie(grad_y, early_grad)
    early_share = lax.psum_scatter(early_grad, "dp", scatter_dimension=0, tiled=True)

    def back(seq, upstream, old):
        def rows_of(width, rows=ROWS):
            return pl.BlockSpec((1, rows, width), lambda i: (seq, blocks - 1 - i, 0))

        per_block = chunks // blocks
        before_spec = pl.BlockSpec(
            (1, 16, inner),
            lambda i: (seq, jnp.maximum((blocks - 1 - i) * (ROWS // 16) - 1, 0), 0),
        )
        shapes = [
            seen((seqs, length, inner), BF),
            seen((seqs, length, states), BF),
            seen((seqs, length, LANES), BF),
            seen((8 * kwidth + 16, inner)),
            seen((16, LANES)),
        ]
        if old is None:
            in_place = (grad_y, conv_bc, step)
            sums = (jnp.zeros(shapes[3].shape, F32), jnp.zeros(shapes[4].shape, F32))
            aliases = {}
        else:
            in_place = old[:3]
            sums = old[3:]
            aliases = {14: 3, 15: 4, 16: 0, 17: 1, 18: 2}
        return pl.pallas_call(
            functools.partial(back_kernel, kwidth),
            grid=(blocks,),
            in_specs=[
                rows_of(inner),
                rows_of(states),
                rows_of(LANES),
                rows_of(LANES),
                rows_of(inner),
                rows_of(inner),
                pl.BlockSpec(
                    (1, per_block, states // 2, inner), lambda i: (seq, blocks - 1 - i, 0, 0)
                ),
                rows_of(inner),
                fixed((8, inner), 1),
                fixed((8, LANES), 1),
                fixed((LANES, inner), 1),
                fixed((2 * LANES, inner), 1),
                fixed((8, inner), 1),
                before_spec,
                fixed(shapes[3].shape, 1),
                fixed(shapes[4].shape, 1),
                any_spec,
                any_spec,
                any_spec,
            ],
            out_specs=[
                rows_of(inner),
                rows_of(states),
                rows_of(LANES),
                fixed(shapes[3].shape, 1),
                fixed(shapes[4].shape, 1),
            ],
            out_shape=shapes,
            scratch_shapes=[
                pltpu.VMEM((states // 2, inner), F32),
                pltpu.VMEM((CHUNK + 8, inner), F32),
                pltpu.VMEM((CHUNK + 16, inner), F32),
            ],
            input_output_aliases=aliases,
            compiler_params=params(1),
            cost_estimate=cost(25 * 10**9, length * inner * 16, length * heads * CHUNK),
            name="back",
        )(
            conv_x,
            conv_bc,
            step,
            cum,
            upstream,
            mixed_y,
            old_states,
            conv_in,
            taps[:, :inner],
            head_rows,
            spread1,
            spread2,
            skip_row,
            conv_in,
            *sums,
            *in_place,
        )

    arrived = lax.ppermute(out_other, "tensor", [(i, i ^ 1) for i in range(tensor)])
    grad_y, out_own, arrived = tie(grad_y, out_own, arrived)
    out_kept, out_leaving = zip(
        *(core_sums(out_own[:, seq], arrived[:, seq]) for seq in range(seqs))
    )
    grad_y, *flat_leaving = tie(grad_y, *sum(out_leaving, []))
    each = columns - 1
    out_leaving = [flat_leaving[i * each : (i + 1) * each] for i in range(seqs)]
    made = back(0, grad_y, None)
    made = back(1, grad_y, made)
    arrivals = [column_sends(sent) for sent in out_leaving]
    grad_in, grad_bc_part, grad_delta, tap_fold, head_fold = back(2, grad_y, made)
    grad_in, *flat_arrivals = tie(grad_in, *sum(arrivals, []))
    arrivals = [flat_arrivals[i * each : (i + 1) * each] for i in range(seqs)]

    bc_chip = chip_total(grad_bc_part)
    in_grad = weight_grad(normed, grad_in).astype(BF)

    in_parts = lax.all_to_all(in_grad, "dp", split_axis=0, concat_axis=0, tiled=True)
    grad_delta, in_grad, bc_chip = tie(grad_delta, in_grad, bc_chip)
    bc_moved = column_total_sends(bc_chip)
    normed_own, normed_other = pl.pallas_call(
        join_kernel,
        grid=(seqs, wide_blocks),
        in_specs=[
            scalar_spec,
            by_rows(inner),
            by_rows(inner),
            by_rows(LANES),
            pl.BlockSpec((model, inner), lambda s, t: (0, 0)),
            pl.BlockSpec((model, inner), lambda s, t: (0, 0)),
            pl.BlockSpec((model, LANES), lambda s, t: (0, (inner + states) // LANES)),
        ],
        out_specs=[partial_spec, partial_spec],
        out_shape=[seen((columns, seqs, length, share), BF)] * 2,
        compiler_params=params(2),
        cost_estimate=cost(33 * 10**9, tokens_here * (2 * model + 4 * inner)),
        name="join",
    )(
        starts,
        grad_gate,
        grad_in,
        grad_delta,
        second_weight,
        first_weight,
        first_weight,
    )
    normed_own, normed_other, bc_moved, in_parts = tie(
        normed_own, normed_other, bc_moved, in_parts
    )
    normed_arrived = lax.ppermute(normed_other, "tensor", [(i, i ^ 1) for i in range(tensor)])
    normed_kept, normed_leaving = core_sums(normed_own, normed_arrived)
    bc_total = finish_total(bc_chip, bc_moved)
    bc_total, *normed_leaving = tie(bc_total, *normed_leaving)
    normed_moved = column_sends(normed_leaving)
    out_sums = []
    for kept, moved in zip(out_kept, arrivals):
        for part in moved:
            kept = kept + part.astype(F32)
        out_sums.append(kept)
    result = (inputs_share + jnp.stack(out_sums)).astype(BF)

    grad_small, bc_tap_fold = pl.pallas_call(
        functools.partial(bc_kernel, kwidth),
        grid=(seqs,),
        in_specs=[per_seq(states), per_seq(states), fixed((8, states), 1), per_seq(LANES)],
        out_specs=[per_seq(states + LANES), fixed((8 * kwidth + 8, states), 1)],
        out_shape=[
            seen((seqs, length, states + LANES), BF),
            seen((8 * kwidth + 8, states)),
        ],
        scratch_shapes=[
            pltpu.VMEM((length + 8, states), F32),
            pltpu.VMEM((length + 8, states), F32),
        ],
        compiler_params=params(1),
        cost_estimate=cost(8 * 10**9, tokens_here * states * 12),
        name="bc_back",
    )(bc_total, bc_pre, taps[:, inner:], grad_delta)
    small_grad = weight_grad(normed, grad_small).astype(BF)
    small_parts = lax.all_to_all(small_grad, "dp", split_axis=0, concat_axis=0, tiled=True)
    early_wide = early_share.astype(F32)
    gate_share = early_wide[:, :inner]
    out_share = early_wide[:, inner:]
    in_share = sum_parts(in_parts)
    small_share = sum_parts(small_parts)
    bc_share = small_share[:, :states]
    dt_share = small_share[:, states : states + heads]
    gate_m = momentum_rate * zx_moment[:, 0, :] + gate_share
    out_m = momentum_rate * out_moment.T + out_share
    in_m = momentum_rate * zx_moment[:, 1, :] + in_share
    bc_m = momentum_rate * bc_moment + bc_share
    dt_m = momentum_rate * dt_moment + dt_share
    early = jnp.concatenate(
        [gate_share + momentum_rate * gate_m, out_share + momentum_rate * out_m], axis=1
    )
    late = jnp.concatenate(
        [in_share + momentum_rate * in_m, bc_share + momentum_rate * bc_m], axis=1
    )
    dt_input = dt_share + momentum_rate * dt_m
    squares = jnp.sum(dt_input * dt_input, axis=0)
    units, slots = gram_units(early, late, squares)
    factors = newton(units, slots)
    bc_rows = lax.dynamic_slice(first_weight, (share_start, inner), (share, states))
    normed_share = normed_kept
    for moved in normed_moved:
        normed_share = normed_share + moved.astype(F32)
    normed_share = normed_share + jnp.einsum(
        "btk,fk->btf", grad_small[:, :, :states], bc_rows, preferred_element_type=F32
    )

    gain_share = lax.dynamic_slice_in_dim(norm_gain, share_start, share, 0)
    weighted = normed_share * gain_share
    gain_grad_share = jnp.sum(normed_share * inputs_share * inv_rms, axis=(0, 1))
    gain_padded = lax.dynamic_update_slice_in_dim(
        jnp.zeros((model,), F32), gain_grad_share, share_start, 0
    )
    inner_rows = jnp.sum(weighted * inputs_share, axis=-1)
    final_sums = tensor_sum(jnp.concatenate([inner_rows.reshape(-1), gain_padded]))
    final_sums, factors = tie(final_sums, factors)
    inner_sum = final_sums[: seqs * length].reshape(seqs, length)
    gain_part = final_sums[seqs * length :]
    upstream_share = lax.dynamic_slice_in_dim(cotangent, share_start, share, 2).astype(F32)
    input_grad = (
        upstream_share
        + inv_rms * weighted
        - inputs_share * inv_rms**3 * (inner_sum / model)[..., None]
    )

    tap_sums = tap_fold.reshape(kwidth + 2, 8, inner).sum(axis=1)
    head_sums = head_fold.reshape(2, 8, LANES).sum(axis=1)[:, :heads]
    skip_grad = tap_sums[kwidth + 1].reshape(heads, head_width).sum(axis=1)
    pieces = [
        tap_sums[: kwidth + 1].reshape(-1),
        gain_fold.sum(axis=0),
        head_sums.reshape(-1),
        skip_grad,
        bc_tap_fold.reshape(kwidth + 1, 8, states).sum(axis=1).reshape(-1),
        gain_part,
    ]
    flat = dp_sum(jnp.concatenate(pieces))
    xpar_count = (kwidth + 2) * inner
    xpar_g = flat[:xpar_count].reshape(kwidth + 2, inner)
    head_g = flat[xpar_count : xpar_count + 3 * heads].reshape(3, heads)
    bcpar_g = flat[xpar_count + 3 * heads : -model].reshape(kwidth + 1, states)
    gain_g = flat[-model:]

    ortho, dt_scale = updates(early, late, factors, slots, heads)
    early_ortho = ortho[:, : 2 * inner]
    late_ortho = ortho[:, 2 * inner :]
    dt_ortho = dt_input * dt_scale
    shrink = 1.0 - matrix_rate * weight_decay
    zx_m = jnp.stack([gate_m, in_m], axis=1)
    zx_new = w_zx * shrink - matrix_rate * jnp.stack(
        [early_ortho[:, :inner], late_ortho[:, :inner]], axis=1
    )
    bc_new = state_proj_weight * shrink - matrix_rate * late_ortho[:, inner:]
    dt_new = step_weight * shrink - matrix_rate * dt_ortho
    out_new = exit_coefficient_matrix * shrink - matrix_rate * early_ortho[:, inner:].T
    gain_m = momentum_rate * gain_moment + gain_g
    xpar_m = momentum_rate * xpar_moment + xpar_g
    bcpar_m = momentum_rate * bcpar_moment + bcpar_g
    head_m = momentum_rate * head_moment + head_g
    gain_new = norm_gain - small_rate * (gain_g + momentum_rate * gain_m)
    xpar_new = x_params - small_rate * (xpar_g + momentum_rate * xpar_m)
    bcpar_new = bc_params - small_rate * (bcpar_g + momentum_rate * bcpar_m)
    head_new = head_params - small_rate * (head_g + momentum_rate * head_m)
    return (
        result,
        input_grad,
        zx_m,
        zx_new,
        bc_m,
        bc_new,
        dt_m,
        dt_new,
        out_m.T,
        out_new,
        gain_m,
        gain_new,
        xpar_m,
        xpar_new,
        bcpar_m,
        bcpar_new,
        head_m,
        head_new,
    )


def solution(mesh):
    return jax.shard_map(
        local,
        mesh=mesh,
        in_specs=(
            P("dp", None, None),
            P("dp", None, None),
            P(),
            P("dp", None, "tensor"),
            P("dp", None),
            P("dp", "tensor"),
            P("tensor", "dp"),
            P(None, "tensor"),
            P(),
            P(None, "tensor"),
            P("dp", None, "tensor"),
            P("dp", None),
            P("dp", "tensor"),
            P("tensor", "dp"),
            P(),
            P(None, "tensor"),
            P(),
            P(None, "tensor"),
        ),
        out_specs=(
            P("dp", None, "tensor"),
            P("dp", None, "tensor"),
            P("dp", None, "tensor"),
            P("dp", None, "tensor"),
            P("dp", None),
            P("dp", None),
            P("dp", "tensor"),
            P("dp", "tensor"),
            P("tensor", "dp"),
            P("tensor", "dp"),
            P(),
            P(),
            P(None, "tensor"),
            P(None, "tensor"),
            P(),
            P(),
            P(None, "tensor"),
            P(None, "tensor"),
        ),
        check_vma=False,
    )
```

```python
import functools

import jax
import jax.numpy as jnp
from jax import lax
from jax.experimental import pallas as pl
from jax.experimental.pallas import tpu as pltpu
from jax.sharding import PartitionSpec as P

BF = jnp.bfloat16
F32 = jnp.float32
CHUNK = 128
LANES = 128
ROWS = 256
PIECE = 64
WIDE_ROWS = 512
VMEM_BYTES = 52 * 1024 * 1024

exact = lax.Precision.HIGHEST
norm_eps = 1e-05
poly_first = 3.4445
poly_second = -4.775
poly_third = 2.0315
momentum_rate = 0.95
matrix_rate = 0.5
weight_decay = 0.1
small_rate = 0.0025


def params(count):
    return pltpu.CompilerParams(
        dimension_semantics=("arbitrary",) * count, vmem_limit_bytes=VMEM_BYTES
    )


def cost(flops, moved, transcendentals=0):
    return pl.CostEstimate(
        flops=flops // 40, bytes_accessed=moved // 40, transcendentals=transcendentals // 40
    )


def sigmoid(value):
    return 0.5 * jnp.tanh(0.5 * value) + 0.5


def dot(left, right):
    return jnp.dot(left, right, preferred_element_type=F32)


def dot_nt(left, right):
    return lax.dot_general(left, right, (((1,), (1,)), ((), ())), preferred_element_type=F32)


def halves(value):
    high = value.astype(BF)
    low = (value - high.astype(F32)).astype(BF)
    return high, low


def spread_dot(value, spread):
    high, low = halves(value)
    return dot(jnp.concatenate([high, low], axis=1), spread)


def gather_dot(value, spread):
    high, low = halves(value)
    return dot_nt(high, spread) + dot_nt(low, spread)


def tri_dot(triangle, value):
    first = value.astype(BF)
    rest = value - first.astype(F32)
    second = rest.astype(BF)
    third = (rest - second.astype(F32)).astype(BF)
    return dot(triangle, first) + dot(triangle, second) + dot(triangle, third)


def flip(value):
    return value.astype(F32).T.astype(BF)


def row_fold(value):
    return value.reshape(-1, 8, value.shape[-1]).sum(axis=0)


def tiles_of(start, stop, step):
    return [(low, min(step, stop - low)) for low in range(start, stop, step)]


def iota(shape, axis):
    return lax.broadcasted_iota(jnp.int32, shape, axis)


def project_kernel(
    kwidth, normed, weight, taps, heads, conv_in, bc_pre, conv_x, conv_bc, step, cum, buffer
):
    inner = conv_in.shape[-1]
    states = bc_pre.shape[-1]
    rows = normed.shape[1]
    block = pl.program_id(1)

    @pl.when(block == 0)
    def _():
        buffer[0:8, :] = jnp.zeros((8, inner + states), F32)

    @pl.when(block > 0)
    def _():
        buffer[0:8, :] = buffer[rows : rows + 8, :]

    data = normed[0]
    for low, width in tiles_of(0, inner, 256) + tiles_of(inner, inner + states, 256):
        cols = slice(low, low + width)
        made = dot(data, weight[:, cols])
        buffer[8 : 8 + rows, cols] = made
        for top in range(0, rows, PIECE):
            for left in range(low, low + width, LANES):
                here = slice(left, left + LANES)
                kept = buffer[8 + top : 8 + top + PIECE, here]
                total = taps[kwidth : kwidth + 1, here] + taps[kwidth - 1 : kwidth, here] * kept
                for offset in range(kwidth - 1):
                    start = 9 - kwidth + offset + top
                    total = total + taps[offset : offset + 1, here] * (
                        buffer[start : start + PIECE, here]
                    )
                active = (total * sigmoid(total)).astype(BF)
                span = slice(top, top + PIECE)
                if left < inner:
                    conv_in[0, span, here] = kept.astype(BF)
                    conv_x[0, span, here] = active
                else:
                    own = slice(left - inner, left - inner + LANES)
                    bc_pre[0, span, own] = kept
                    conv_bc[0, span, own] = active
    delta = dot(data, weight[:, inner + states :]) + heads[1:2, :]
    size = jnp.maximum(delta, 0.0) + jnp.log1p(jnp.exp(-jnp.abs(delta)))
    decay = -size * jnp.exp(heads[0:1, :])
    step[0] = size
    lower = (iota((CHUNK, CHUNK), 0) >= iota((CHUNK, CHUNK), 1)).astype(F32).astype(BF)
    for low in range(0, rows, CHUNK):
        cum[0, low : low + CHUNK, :] = tri_dot(lower, decay[low : low + CHUNK, :])


def scan_kernel(conv_x, conv_bc, step, cum, spread2, skip, y, states, state):
    inner = conv_x.shape[-1]
    width = conv_bc.shape[-1] // 2
    state[...] = jnp.zeros_like(state)
    causal = iota((CHUNK, CHUNK), 0) >= iota((CHUNK, CHUNK), 1)
    first = iota((CHUNK, LANES), 1) < LANES // 2
    spread = spread2[...]

    def body(index, carry):
        rows = pl.ds(pl.multiple_of(index * CHUNK, CHUNK), CHUNK)
        value = conv_x[0, rows, :]
        b_part = conv_bc[0, rows, :width]
        c_part = conv_bc[0, rows, width:]
        running = cum[0, rows, :]
        size = step[0, rows, :]
        state_low = state[...].astype(BF)
        states[0, index] = state_low
        scores = dot_nt(c_part, b_part)
        carried = dot(c_part, state_low)
        grow = spread_dot(jnp.exp(running), spread)
        tail = spread_dot(size * jnp.exp(running[CHUNK - 1 : CHUNK, :] - running), spread)
        keys = (running - jnp.log(size)).T
        for pair in range(inner // LANES):
            cols = slice(pair * LANES, (pair + 1) * LANES)
            pair_x = value[:, cols]
            stacked = []
            for head in (2 * pair, 2 * pair + 1):
                gap = running[:, head : head + 1] - keys[head : head + 1, :]
                stacked.append(jnp.where(causal, jnp.exp(gap) * scores, 0.0).astype(BF))
            parts = dot(jnp.concatenate(stacked, axis=0), pair_x)
            y[0, rows, cols] = (
                jnp.where(first, parts[:CHUNK], parts[CHUNK:])
                + carried[:, cols] * grow[:, cols]
                + skip[0:1, cols] * pair_x.astype(F32)
            )
        weighted = (value.astype(F32) * tail).astype(BF)
        state[...] = state[...] * grow[CHUNK - 1 : CHUNK, :] + dot(flip(b_part), weighted)
        return carry

    lax.fori_loop(0, conv_x.shape[1] // CHUNK, body, 0)


def gate_kernel(normed, cotangent, weight, y, gain, gate_pre, grad_mixed, stats):
    inner = y.shape[-1]
    rows = normed.shape[1]
    data = normed[0]
    upstream = cotangent[0]
    squares = [jnp.zeros((PIECE, LANES), F32) for _ in range(rows // PIECE)]
    products = [jnp.zeros((PIECE, LANES), F32) for _ in range(rows // PIECE)]
    for low, width in tiles_of(0, inner, 256):
        cols = slice(low, low + width)
        pre_all = dot(data, weight[:, cols])
        grad_all = dot(upstream, weight[:, inner + low : inner + low + width])
        gate_pre[0, :, cols] = pre_all.astype(BF)
        grad_mixed[0, :, cols] = grad_all.astype(BF)
        for piece in range(rows // PIECE):
            span = slice(piece * PIECE, (piece + 1) * PIECE)
            for left in range(0, width, LANES):
                here = slice(low + left, low + left + LANES)
                pre = pre_all[span, left : left + LANES]
                gated = y[0, span, here] * pre * sigmoid(pre)
                squares[piece] = squares[piece] + gated * gated
                products[piece] = products[piece] + (
                    grad_all[span, left : left + LANES] * gain[0:1, here] * gated
                )
    squares = jnp.concatenate(squares, axis=0)
    products = jnp.concatenate(products, axis=0)
    lane = iota((rows, LANES), 1)
    both = jnp.where(
        lane == 0,
        jnp.sum(squares, axis=1, keepdims=True),
        jnp.where(lane == 1, jnp.sum(products, axis=1, keepdims=True), 0.0),
    )
    stats[0] = both.T[0:8, :]


def mix_kernel(
    starts,
    y,
    gate_pre,
    grad_mixed,
    scales,
    gain,
    weight,
    mixed,
    grad_y,
    grad_gate,
    own_core,
    other_core,
    gain_sum,
):
    inner = y.shape[-1]
    rows = y.shape[1]

    @pl.when((pl.program_id(0) == 0) & (pl.program_id(1) == 0))
    def _():
        gain_sum[...] = jnp.zeros_like(gain_sum)

    by_row = scales[0].T
    inverse = by_row[:, 0:1]
    slope = by_row[:, 1:2]
    for low in range(0, inner, LANES):
        cols = slice(low, low + LANES)
        gain_here = gain[0:1, cols]
        folded = jnp.zeros((8, LANES), F32)
        for top in range(0, rows, PIECE):
            span = slice(top, top + PIECE)
            value = y[0, span, cols]
            pre = gate_pre[0, span, cols].astype(F32)
            upstream = grad_mixed[0, span, cols].astype(F32)
            logistic = sigmoid(pre)
            act = pre * logistic
            gated = value * act
            scaled = gated * inverse[span]
            folded = folded + row_fold(upstream * scaled)
            mixed[0, span, cols] = (scaled * gain_here).astype(BF)
            grad_gated = inverse[span] * (upstream * gain_here) - gated * slope[span]
            grad_y[0, span, cols] = (grad_gated * act).astype(BF)
            grad_gate[0, span, cols] = (
                grad_gated * value * (logistic * (1.0 + pre * (1.0 - logistic)))
            ).astype(BF)
        gain_sum[:, cols] += folded
    data = mixed[0]
    share = own_core.shape[-1]
    columns = own_core.shape[0]
    for part in range(2 * columns):
        rows = pl.ds(pl.multiple_of(starts[part], share), share)
        made = dot_nt(data, weight[rows, :]).astype(BF)
        if part < columns:
            own_core[part, 0] = made
        else:
            other_core[part - columns, 0] = made


def back_kernel(
    kwidth,
    conv_x,
    conv_bc,
    step,
    cum,
    grad_y,
    y,
    states,
    conv_in,
    taps,
    heads,
    spread1,
    spread2,
    skip,
    in_before,
    old_taps,
    old_heads,
    after_in,
    after_bc,
    after_delta,
    grad_in,
    grad_bc,
    grad_delta,
    tap_sums,
    head_sums,
    grad_state,
    back_buffer,
    in_buffer,
):
    inner = conv_x.shape[-1]
    width = conv_bc.shape[-1] // 2
    chunks = conv_x.shape[1] // CHUNK
    step_index = pl.program_id(0)
    first_block = step_index == pl.num_programs(0) - 1

    @pl.when(step_index == 0)
    def _():
        tap_sums[...] = old_taps[...]
        head_sums[...] = old_heads[...]
        grad_state[...] = jnp.zeros_like(grad_state)
        back_buffer[0:8, :] = jnp.zeros((8, inner), F32)

    anti = iota((CHUNK, CHUNK), 0) <= iota((CHUNK, CHUNK), 1)
    upper = anti.astype(F32).astype(BF)
    first = iota((CHUNK, LANES), 1) < LANES // 2
    rate = jnp.exp(heads[0:1, :])
    spread = spread2[...]
    gather = spread1[...]

    for index in reversed(range(chunks)):
        rows = slice(index * CHUNK, (index + 1) * CHUNK)
        value = conv_x[0, rows, :]
        b_part = conv_bc[0, rows, :width]
        c_part = conv_bc[0, rows, width:]
        running = cum[0, rows, :]
        size = step[0, rows, :]
        upstream = grad_y[0, rows, :]
        old_state = states[0, index]
        state_grad = grad_state[...]
        state_grad_low = state_grad.astype(BF)
        scores = dot_nt(b_part, c_part)
        reach = dot(b_part, state_grad_low)
        grow = spread_dot(jnp.exp(running), spread)
        tail = spread_dot(size * jnp.exp(running[CHUNK - 1 : CHUNK, :] - running), spread)
        grown = (upstream.astype(F32) * grow).astype(BF)
        weighted = (value.astype(F32) * tail).astype(BF)
        grad_c = dot_nt(grown, old_state)
        grad_b = dot_nt(weighted, state_grad_low)
        last_grow = grow[CHUNK - 1 : CHUNK, :]
        grad_state[...] = state_grad * last_grow + dot(flip(c_part), grown)
        kept = row_fold(old_state.astype(F32) * state_grad) * last_grow
        queries = running.T
        keys = running - jnp.log(size)
        score_grad = jnp.zeros((CHUNK, CHUNK), F32)
        flow_parts = []
        pull_parts = []
        end_parts = []
        if index > 0:
            in_buffer[0:16, :] = conv_in[0, index * CHUNK - 16 : index * CHUNK, :].astype(F32)
        else:
            in_buffer[0:16, :] = jnp.where(first_block, 0.0, in_before[0].astype(F32))
        in_buffer[16 : 16 + CHUNK, :] = conv_in[0, rows, :].astype(F32)
        back_buffer[CHUNK : CHUNK + 8, :] = back_buffer[0:8, :]
        for pair in range(inner // LANES):
            cols = slice(pair * LANES, (pair + 1) * LANES)
            pair_x = value[:, cols]
            pair_up = upstream[:, cols]
            kernels = []
            for head in (2 * pair, 2 * pair + 1):
                gap = queries[head : head + 1, :] - keys[:, head : head + 1]
                kernels.append(jnp.where(anti, jnp.exp(gap), 0.0))
            nothing = jnp.zeros_like(pair_x)
            own_x = jnp.concatenate(
                [jnp.where(first, pair_x, nothing), jnp.where(first, nothing, pair_x)], axis=0
            )
            products = dot_nt(own_x, pair_up)
            score_grad = (
                score_grad + kernels[0] * products[:CHUNK] + kernels[1] * products[CHUNK:]
            )
            stacked = [(kernel * scores).astype(BF) for kernel in kernels]
            parts = dot(jnp.concatenate(stacked, axis=0), pair_up)
            x_wide = pair_x.astype(F32)
            up_wide = pair_up.astype(F32)
            far = reach[:, cols] * tail[:, cols]
            inside = jnp.where(first, parts[:CHUNK], parts[CHUNK:]) + far
            skip_row = skip[0:1, cols]
            pull = x_wide * inside
            pull_parts.append(pull)
            flow_parts.append(up_wide * (y[0, rows, cols] - skip_row * x_wide) - pull)
            end_parts.append(row_fold(x_wide * far) + kept[:, cols])
            grad_x = inside + skip_row * up_wide
            now = in_buffer[16 : 16 + CHUNK, cols]
            shifted = [
                in_buffer[17 - kwidth + offset : 17 - kwidth + offset + CHUNK, cols]
                for offset in range(kwidth - 1)
            ] + [now]
            total = taps[kwidth : kwidth + 1, cols]
            for offset in range(kwidth):
                total = total + taps[offset : offset + 1, cols] * shifted[offset]
            logistic = sigmoid(total)
            error = grad_x * (logistic * (1.0 + total * (1.0 - logistic)))
            back_buffer[0:CHUNK, cols] = error
            for offset in range(kwidth):
                tap_sums[8 * offset : 8 * offset + 8, cols] += row_fold(error * shifted[offset])
            tap_sums[8 * kwidth : 8 * kwidth + 8, cols] += row_fold(error)
            tap_sums[8 * kwidth + 8 : 8 * kwidth + 16, cols] += row_fold(x_wide * up_wide)
            moved = taps[kwidth - 1 : kwidth, cols] * error
            for offset in range(kwidth - 1):
                start = kwidth - 1 - offset
                moved = moved + (
                    taps[offset : offset + 1, cols] * back_buffer[start : start + CHUNK, cols]
                )
            grad_in[0, rows, cols] = moved.astype(BF)
        score_low = score_grad.astype(BF)
        grad_bc[0, rows, :width] = (grad_b + dot(score_low, c_part)).astype(BF)
        grad_bc[0, rows, width:] = (grad_c + dot(flip(score_grad), b_part)).astype(BF)
        flow = gather_dot(jnp.concatenate(flow_parts, axis=1), gather)
        pull = gather_dot(jnp.concatenate(pull_parts, axis=1), gather)
        ends = gather_dot(jnp.concatenate(end_parts, axis=1), gather)
        decay_grad = tri_dot(upper, flow) + jnp.sum(ends, axis=0, keepdims=True)
        size_grad = pull / jnp.maximum(size, 1e-37) - rate * decay_grad
        small = size * (1.0 - size * (0.5 - size * (1.0 / 6.0)))
        delta_grad = size_grad * jnp.where(size < 0.01, small, 1.0 - jnp.exp(-size))
        grad_delta[0, rows, :] = delta_grad.astype(BF)
        head_sums[0:8, :] += row_fold(decay_grad * (-size * rate))
        head_sums[8:16, :] += row_fold(delta_grad)


def join_kernel(
    starts, grad_gate, grad_in, grad_delta, gate_weight, in_weight, step_weight, own_core, other_core
):
    share = own_core.shape[-1]
    columns = own_core.shape[0]
    for part in range(2 * columns):
        rows = pl.ds(pl.multiple_of(starts[part], share), share)
        total = dot_nt(grad_gate[0], gate_weight[rows, :])
        total = total + dot_nt(grad_in[0], in_weight[rows, :])
        total = total + dot_nt(grad_delta[0], step_weight[rows, :])
        if part < columns:
            own_core[part, 0] = total.astype(BF)
        else:
            other_core[part - columns, 0] = total.astype(BF)


def bc_kernel(kwidth, summed, pre, taps, grad_delta, grad_small, tap_sums, before, later):
    length = pre.shape[1]
    width = pre.shape[2]

    @pl.when(pl.program_id(0) == 0)
    def _():
        tap_sums[...] = jnp.zeros_like(tap_sums)

    before[0:8, :] = jnp.zeros((8, width), F32)
    before[8 : 8 + length, :] = pre[0]
    later[length : length + 8, :] = jnp.zeros((8, width), F32)
    for left in range(0, width, LANES):
        here = slice(left, left + LANES)

        folds = [jnp.zeros((8, LANES), F32) for _ in range(kwidth + 1)]
        for top in range(0, length, PIECE):
            span = slice(top, top + PIECE)
            shifted = [
                before[top + 9 - kwidth + offset : top + 9 - kwidth + offset + PIECE, here]
                for offset in range(kwidth)
            ]
            total = taps[kwidth : kwidth + 1, here]
            for offset in range(kwidth):
                total = total + taps[offset : offset + 1, here] * shifted[offset]
            logistic = sigmoid(total)
            error = summed[0, span, here].astype(F32) * (
                logistic * (1.0 + total * (1.0 - logistic))
            )
            later[span, here] = error
            for offset in range(kwidth):
                folds[offset] = folds[offset] + row_fold(error * shifted[offset])
            folds[kwidth] = folds[kwidth] + row_fold(error)
        for offset in range(kwidth + 1):
            tap_sums[8 * offset : 8 * offset + 8, here] += folds[offset]
        for top in range(0, length, PIECE):
            moved = taps[kwidth - 1 : kwidth, here] * later[top : top + PIECE, here]
            for offset in range(kwidth - 1):
                start = top + kwidth - 1 - offset
                moved = moved + taps[offset : offset + 1, here] * later[start : start + PIECE, here]
            grad_small[0, top : top + PIECE, here] = moved.astype(BF)
    grad_small[0, :, width:] = grad_delta[0]


def block_mask():
    half = LANES // 2
    return (iota((LANES, LANES), 0) < half) == (iota((LANES, LANES), 1) < half)


def pair_pack(matrix):
    half = LANES // 2
    return jnp.where(iota((half, LANES), 1) < half, matrix[:half], matrix[half:])


def pair_unpack(unit):
    half = LANES // 2
    left = iota((half, LANES), 1) < half
    return jnp.concatenate([jnp.where(left, unit, 0.0), jnp.where(left, 0.0, unit)], axis=0)


def gram_kernel(slots, first, second, squares, units):
    half = LANES // 2
    pairs, wholes, single = slots
    units[...] = jnp.zeros_like(units)
    split = first.shape[1] // LANES
    for index in range(pairs + len(wholes)):
        source, at = (first, index) if index < split else (second, index - split)
        part = source[:, at * LANES : (at + 1) * LANES]
        made = jnp.dot(part.T, part, precision=exact, preferred_element_type=F32)
        if index < pairs:
            units[index] = pair_pack(made)
        else:
            slot = wholes[index - pairs]
            units[slot] = made[:half]
            units[slot + 1] = made[half:]
    units[single, 0:8, :] = squares[...]


def newton_kernel(parts, kinds, result):
    half = LANES // 2
    same = block_mask()
    eye = (iota((LANES, LANES), 0) == iota((LANES, LANES), 1)).astype(F32)
    low_row = iota((LANES, 1), 0) < half
    low_col = iota((1, LANES), 1) < half

    def mul(left, right):
        return jnp.dot(left, right, precision=exact, preferred_element_type=F32)

    count = result.shape[0]
    sums = []
    for index in range(count):
        total = parts[0, index]
        for source in range(1, parts.shape[0]):
            total = total + parts[source, index]
        sums.append(total)
    whole = kinds[0:1, :] > 0.5
    is_whole = whole[:, 0:1]
    grams = [pair_unpack(unit) for unit in sums]
    grams[0] = jnp.where(whole, jnp.concatenate(sums[:2], axis=0), grams[0])
    scales = []
    for index in range(count):
        diagonal = jnp.sum(grams[index] * eye, axis=0, keepdims=True)
        low_trace = jnp.sum(jnp.where(low_col, diagonal, 0.0), axis=1, keepdims=True)
        high_trace = jnp.sum(jnp.where(low_col, 0.0, diagonal), axis=1, keepdims=True)
        if index == 0:
            both = low_trace + high_trace
            low_trace = jnp.where(is_whole, both, low_trace)
            high_trace = jnp.where(is_whole, both, high_trace)
        low_scale = 1.0 / (jnp.sqrt(low_trace) + 1e-07)
        high_scale = 1.0 / (jnp.sqrt(high_trace) + 1e-07)
        scale_row = jnp.where(low_row, low_scale, high_scale)
        scale_col = jnp.where(low_col, low_scale, high_scale)
        grams[index] = grams[index] * scale_row * scale_col
        scales.append(scale_row)
    totals = [None] * count
    for sweep in range(5):
        squares = [mul(gram, gram) for gram in grams]
        factors = [
            poly_first * eye + poly_second * gram + poly_third * square
            for gram, square in zip(grams, squares)
        ]
        totals = [
            scale * factor if sweep == 0 else mul(total, factor)
            for scale, total, factor in zip(scales, totals, factors)
        ]
        if sweep < 4:
            halfway = [mul(factor, gram) for factor, gram in zip(factors, grams)]
            grams = [mul(left, factor) for left, factor in zip(halfway, factors)]
    for index in range(count):
        made = pair_pack(totals[index])
        if index < 2:
            here = totals[0][:half] if index == 0 else totals[0][half:]
            made = jnp.where(whole, here, made)
        length = sums[index]
        scale = 1.0 / (jnp.sqrt(length) + 1e-07)
        length = length * scale * scale
        for sweep in range(5):
            step = poly_first + length * (poly_second + poly_third * length)
            scale = scale * step
            length = length * step * step
        single = kinds[8 + index : 9 + index, :] > 0.5
        result[index] = jnp.where(single, scale, made).astype(BF)


def apply_kernel(slots, first, second, units, made):
    pairs, wholes, single = slots
    split = first.shape[1] // LANES
    for index in range(pairs + len(wholes)):
        source, at = (first, index) if index < split else (second, index - split)
        if index < pairs:
            factor = pair_unpack(units[index].astype(F32))
        else:
            slot = wholes[index - pairs]
            factor = jnp.concatenate([units[slot], units[slot + 1]], axis=0).astype(F32)
        made[:, index * LANES : (index + 1) * LANES] = jnp.dot(
            source[:, at * LANES : (at + 1) * LANES],
            factor,
            precision=exact,
            preferred_element_type=F32,
        )


def whole_call(kernel, shapes, *operands):
    return pl.pallas_call(
        kernel,
        out_shape=shapes,
        compiler_params=pltpu.CompilerParams(vmem_limit_bytes=VMEM_BYTES),
    )(*operands)


def seen(shape, dtype=F32):
    return jax.ShapeDtypeStruct(shape, dtype)


def by_rows(width, rows=WIDE_ROWS):
    return pl.BlockSpec((1, rows, width), lambda s, t: (s, t, 0))


def fixed(shape, count):
    if count == 2:
        return pl.BlockSpec(shape, lambda s, t: (0,) * len(shape))
    return pl.BlockSpec(shape, lambda s: (0,) * len(shape))


def pad_rows(array, rows=8):
    return jnp.pad(array, ((0, rows - array.shape[0]), (0, 0)))


def pad_cols(array, cols):
    return jnp.pad(array, ((0, 0), (0, cols - array.shape[1])))


def copy_to_all(array, axis):
    count = lax.axis_size(axis)
    return lax.all_to_all(
        jnp.broadcast_to(array, (count,) + array.shape), axis, split_axis=0, concat_axis=0, tiled=True
    )


def block_starts(share):
    columns = lax.axis_size("tensor") // 2
    me = lax.axis_index("tensor")
    order = (me // 2 + jnp.arange(columns)) % columns
    return (
        share * jnp.concatenate([2 * order + me % 2, 2 * order + 1 - me % 2])
    ).astype(jnp.int32)


def core_sums(own, arrived):
    kept = own[0].astype(F32) + arrived[0].astype(F32)
    leaving = [
        (own[shift].astype(F32) + arrived[shift].astype(F32)).astype(BF)
        for shift in range(1, own.shape[0])
    ]
    return kept, leaving


def core_phase(own, other):
    count = lax.axis_size("tensor")
    return core_sums(own, lax.ppermute(other, "tensor", [(i, i ^ 1) for i in range(count)]))


def column_sends(leaving):
    count = lax.axis_size("tensor")
    columns = count // 2
    return [
        lax.ppermute(
            sent,
            "tensor",
            [(i, ((i // 2 + shift) % columns) * 2 + i % 2) for i in range(count)],
        )
        for shift, sent in enumerate(leaving, 1)
    ]


def column_phase(kept, leaving):
    for moved in column_sends(leaving):
        kept = kept + moved.astype(F32)
    return kept


def tensor_sum(value):
    count = lax.axis_size("tensor")
    step = 1
    while step < count:
        value = value + lax.ppermute(value, "tensor", [(i, i ^ step) for i in range(count)])
        step *= 2
    return value


def after(value, *others):
    return lax.optimization_barrier((value,) + others)[0]


def tie(*values):
    return lax.optimization_barrier(values)


def gather_rows(shard):
    count = lax.axis_size("dp")
    if count != 8:
        return lax.all_gather(shard, "dp", axis=0, tiled=True), shard, shard
    rows = shard.shape[0]
    me = lax.axis_index("dp")
    z = me // 2
    y = me % 2
    result = jnp.zeros((9 * rows, shard.shape[1]), shard.dtype)
    swap = [(i, i ^ 1) for i in range(count)]

    def place(result, piece, z_from, y_from):
        there = (z_from >= 0) & (z_from < 4)
        start = jnp.where(there, (z_from * 2 + y_from) * rows, 8 * rows)
        return lax.dynamic_update_slice_in_dim(result, piece, start, 0)

    other = lax.ppermute(shard, "dp", swap)
    result = place(result, shard, z, y)
    up = down = shard
    for step in range(1, 4):
        up = lax.ppermute(
            up, "dp", [(2 * i + j, 2 * i + 2 + j) for i in range(step - 1, 3) for j in range(2)]
        )
        down = lax.ppermute(
            down, "dp", [(2 * i + j, 2 * i - 2 + j) for i in range(1, 5 - step) for j in range(2)]
        )
        if step == 1:
            up, down, other = tie(up, down, other)
        result = place(place(result, up, z - step, y), down, z + step, y)
    leaving = jnp.concatenate(
        [
            lax.dynamic_slice_in_dim(result, ((z ^ k) * 2 + y) * rows, rows, 0)
            for k in range(1, 4)
        ],
        axis=0,
    )
    arrived = lax.ppermute(leaving, "dp", swap)
    result = place(result, other, z, 1 - y)
    for k in range(1, 4):
        result = place(result, arrived[(k - 1) * rows : k * rows], z ^ k, 1 - y)
    return result, up, down


def sum_parts(parts):
    count = lax.axis_size("dp")
    return parts.reshape(count, -1, parts.shape[1]).astype(F32).sum(axis=0)


def add_low(left, right):
    return (left.astype(F32) + right.astype(F32)).astype(BF)


def chip_total(value):
    count = lax.axis_size("tensor")
    half = value.shape[1] // 2
    arrived = lax.ppermute(value, "tensor", [(i, i ^ 1) for i in range(count)])
    start = lax.axis_index("tensor") % 2 * half
    return add_low(
        lax.dynamic_slice_in_dim(value, start, half, 1),
        lax.dynamic_slice_in_dim(arrived, start, half, 1),
    )


def column_total_sends(part):
    count = lax.axis_size("tensor")
    return lax.ppermute(part, "tensor", [(i, i ^ 2) for i in range(count)])


def finish_total(part, moved):
    count = lax.axis_size("tensor")
    part = add_low(part, moved)
    step = 4
    while step < count:
        part = add_low(part, lax.ppermute(part, "tensor", [(i, i ^ step) for i in range(count)]))
        step *= 2
    other = lax.ppermute(part, "tensor", [(i, i ^ 1) for i in range(count)])
    first = lax.axis_index("tensor") % 2 == 0
    return jnp.concatenate(
        [jnp.where(first, part, other), jnp.where(first, other, part)], axis=1
    )


def dp_sum(value):
    count = lax.axis_size("dp")
    step = 1
    while step < count:
        value = value + lax.ppermute(value, "dp", [(i, i ^ step) for i in range(count)])
        step *= 2
    return value


def gram_units(first, second, squares):
    dp = lax.axis_size("dp")
    half = LANES // 2
    pairs = (first.shape[1] + second.shape[1]) // LANES - 2
    each = max(2, -(-pairs // (dp - 2)))
    wholes = ((dp - 2) * each, (dp - 1) * each)
    single = wholes[0] + 2 if each > 2 else wholes[0] - each
    slots = (pairs, wholes, single)
    square_rows = pad_rows(pad_cols(squares[None], LANES))
    units = whole_call(
        functools.partial(gram_kernel, slots),
        seen((dp * each, half, LANES)),
        first,
        second,
        square_rows,
    )
    return units, slots


def newton(units, slots):
    dp = lax.axis_size("dp")
    half = LANES // 2
    each = units.shape[0] // dp
    single = slots[2]
    parts = lax.all_to_all(units, "dp", split_axis=0, concat_axis=0, tiled=True)
    me = lax.axis_index("dp")
    kinds = jnp.concatenate(
        [
            jnp.broadcast_to((me >= dp - 2).astype(F32), (8, LANES)),
            jnp.broadcast_to(
                (me * each + jnp.arange(8) == single).astype(F32)[:, None], (8, LANES)
            ),
        ],
        axis=0,
    )
    factors = whole_call(
        newton_kernel, seen((each, half, LANES), BF), parts.reshape(dp, each, half, LANES), kinds
    )
    return factors


def updates(first, second, factors, slots, count):
    dp = lax.axis_size("dp")
    half = LANES // 2
    each = factors.shape[0]
    single = slots[2]
    factors = copy_to_all(factors, "dp").reshape(dp * each, half, LANES)
    made = whole_call(
        functools.partial(apply_kernel, slots),
        seen((first.shape[0], first.shape[1] + second.shape[1])),
        first,
        second,
        factors,
    )
    return made, factors[single, 0, :count].astype(F32)


def local(
    tokens,
    cotangent,
    norm_gain,
    w_zx,
    state_proj_weight,
    step_weight,
    exit_coefficient_matrix,
    x_params,
    bc_params,
    head_params,
    zx_moment,
    bc_moment,
    dt_moment,
    out_moment,
    gain_moment,
    xpar_moment,
    bcpar_moment,
    head_moment,
):
    kwidth = bc_params.shape[0] - 1
    heads = head_params.shape[1]
    inner = x_params.shape[1]
    head_width = inner // heads
    states = bc_params.shape[1]
    seqs, length, model = tokens.shape
    tensor = lax.axis_size("tensor")
    tensor_index = lax.axis_index("tensor")
    share = model // tensor
    share_start = tensor_index * share
    whole_inner = inner * tensor
    blocks = length // ROWS
    wide_blocks = length // WIDE_ROWS
    chunks = length // CHUNK
    tokens_here = seqs * length

    first_weight, last_up, last_down = gather_rows(
        jnp.concatenate(
            [w_zx[:, 1, :], state_proj_weight, pad_cols(step_weight, LANES)], axis=1
        ).astype(BF)
    )
    second_part = jnp.concatenate([w_zx[:, 0, :], exit_coefficient_matrix.T], axis=1).astype(BF)
    second_weight = lax.all_gather(
        after(second_part, last_up, last_down), "dp", axis=0, tiled=True
    )
    wide = after(tokens, last_up, last_down, second_part).astype(F32)
    inv_rms = lax.rsqrt(jnp.mean(wide * wide, axis=-1, keepdims=True) + norm_eps)
    normed = lax.optimization_barrier((wide * inv_rms * norm_gain).astype(BF))
    any_spec = pl.BlockSpec(memory_space=pl.ANY)

    starts = block_starts(share)

    taps = pad_rows(jnp.concatenate([x_params[: kwidth + 1], bc_params], axis=1))
    head_rows = pad_rows(pad_cols(head_params, LANES))
    lane_head = jnp.arange(inner) // head_width
    spread1 = (jnp.arange(LANES)[:, None] == lane_head[None, :]).astype(BF)
    spread2 = jnp.concatenate([spread1, spread1], axis=0)
    skip_row = jnp.broadcast_to(jnp.repeat(head_params[2], head_width)[None], (8, inner))
    gain_row = jnp.broadcast_to(x_params[kwidth + 1][None], (8, inner))

    first_cols = first_weight.shape[1]
    conv_in, bc_pre, conv_x, conv_bc, step, cum = pl.pallas_call(
        functools.partial(project_kernel, kwidth),
        grid=(seqs, wide_blocks),
        in_specs=[
            by_rows(model),
            fixed((model, first_cols), 2),
            fixed((8, inner + states), 2),
            fixed((8, LANES), 2),
        ],
        out_specs=[
            by_rows(inner),
            by_rows(states),
            by_rows(inner),
            by_rows(states),
            by_rows(LANES),
            by_rows(LANES),
        ],
        out_shape=[
            seen((seqs, length, inner), BF),
            seen((seqs, length, states)),
            seen((seqs, length, inner), BF),
            seen((seqs, length, states), BF),
            seen((seqs, length, LANES)),
            seen((seqs, length, LANES)),
        ],
        scratch_shapes=[pltpu.VMEM((WIDE_ROWS + 8, inner + states), F32)],
        compiler_params=params(2),
        cost_estimate=cost(
            28 * 10**9, tokens_here * (model + 3 * inner) * 2
        ),
        name="project",
    )(normed, first_weight, taps, head_rows)

    def per_seq(width):
        return pl.BlockSpec((1, length, width), lambda s: (s, 0, 0))

    state_spec = pl.BlockSpec((1, chunks, states // 2, inner), lambda s: (s, 0, 0, 0))
    mixed_y, old_states = pl.pallas_call(
        scan_kernel,
        grid=(seqs,),
        in_specs=[
            per_seq(inner),
            per_seq(states),
            per_seq(LANES),
            per_seq(LANES),
            fixed((2 * LANES, inner), 1),
            fixed((8, inner), 1),
        ],
        out_specs=[per_seq(inner), state_spec],
        out_shape=[
            seen((seqs, length, inner)),
            seen((seqs, chunks, states // 2, inner), BF),
        ],
        scratch_shapes=[pltpu.VMEM((states // 2, inner), F32)],
        compiler_params=params(1),
        cost_estimate=cost(
            20 * 10**9, tokens_here * inner * 8, tokens_here * heads * CHUNK
        ),
        name="scan",
    )(conv_x, conv_bc, step, cum, spread2, skip_row)

    stats_spec = pl.BlockSpec((1, 8, WIDE_ROWS), lambda s, t: (s, 0, t))
    gate_pre, grad_mixed, stats = pl.pallas_call(
        gate_kernel,
        grid=(seqs, wide_blocks),
        in_specs=[
            by_rows(model),
            by_rows(model),
            fixed((model, 2 * inner), 2),
            by_rows(inner),
            fixed((8, inner), 2),
        ],
        out_specs=[by_rows(inner), by_rows(inner), stats_spec],
        out_shape=[
            seen((seqs, length, inner), BF),
            seen((seqs, length, inner), BF),
            seen((seqs, 8, length)),
        ],
        compiler_params=params(2),
        cost_estimate=cost(27 * 10**9, tokens_here * (4 * model + 8 * inner)),
        name="gate",
    )(normed, cotangent, second_weight, mixed_y, gain_row)

    sums = tensor_sum(stats[:, :2])
    inverse = lax.rsqrt(sums[:, 0] / whole_inner + norm_eps)
    slope = inverse**3 * (sums[:, 1] / whole_inner)
    scales = jnp.pad(jnp.stack([inverse, slope], axis=1), ((0, 0), (0, 6), (0, 0)))

    columns = tensor // 2
    partial_spec = pl.BlockSpec((columns, 1, WIDE_ROWS, share), lambda s, t: (0, s, t, 0))
    scalar_spec = pl.BlockSpec(memory_space=pltpu.SMEM)
    blended, grad_y, grad_gate, out_own, out_other, gain_fold = pl.pallas_call(
        mix_kernel,
        grid=(seqs, wide_blocks),
        in_specs=[
            scalar_spec,
            by_rows(inner),
            by_rows(inner),
            by_rows(inner),
            stats_spec,
            fixed((8, inner), 2),
            pl.BlockSpec((model, inner), lambda s, t: (0, 1)),
        ],
        out_specs=[
            by_rows(inner),
            by_rows(inner),
            by_rows(inner),
            partial_spec,
            partial_spec,
            fixed((8, inner), 2),
        ],
        out_shape=[
            seen((seqs, length, inner), BF),
            seen((seqs, length, inner), BF),
            seen((seqs, length, inner), BF),
            seen((columns, seqs, length, share), BF),
            seen((columns, seqs, length, share), BF),
            seen((8, inner)),
        ],
        compiler_params=params(2),
        cost_estimate=cost(
            28 * 10**9, tokens_here * (2 * model + 14 * inner)
        ),
        name="mix",
    )(starts, mixed_y, gate_pre, grad_mixed, scales, gain_row, second_weight)

    inputs_share = lax.dynamic_slice_in_dim(tokens, share_start, share, 2).astype(F32)

    def weight_grad(left, right):
        return jnp.einsum("std,stu->du", left, right, preferred_element_type=F32)

    out_grad = weight_grad(cotangent, blended).astype(BF)
    grad_gate, out_grad = tie(grad_gate, out_grad)
    gate_grad = weight_grad(normed, grad_gate).astype(BF)
    early_grad = jnp.concatenate([gate_grad, out_grad], axis=1)
    grad_y, early_grad = tie(grad_y, early_grad)
    early_share = lax.psum_scatter(early_grad, "dp", scatter_dimension=0, tiled=True)

    def back(seq, upstream, old):
        def rows_of(width, rows=ROWS):
            return pl.BlockSpec((1, rows, width), lambda i: (seq, blocks - 1 - i, 0))

        per_block = chunks // blocks
        before_spec = pl.BlockSpec(
            (1, 16, inner),
            lambda i: (seq, jnp.maximum((blocks - 1 - i) * (ROWS // 16) - 1, 0), 0),
        )
        shapes = [
            seen((seqs, length, inner), BF),
            seen((seqs, length, states), BF),
            seen((seqs, length, LANES), BF),
            seen((8 * kwidth + 16, inner)),
            seen((16, LANES)),
        ]
        if old is None:
            in_place = (grad_y, conv_bc, step)
            sums = (jnp.zeros(shapes[3].shape, F32), jnp.zeros(shapes[4].shape, F32))
            aliases = {}
        else:
            in_place = old[:3]
            sums = old[3:]
            aliases = {14: 3, 15: 4, 16: 0, 17: 1, 18: 2}
        return pl.pallas_call(
            functools.partial(back_kernel, kwidth),
            grid=(blocks,),
            in_specs=[
                rows_of(inner),
                rows_of(states),
                rows_of(LANES),
                rows_of(LANES),
                rows_of(inner),
                rows_of(inner),
                pl.BlockSpec(
                    (1, per_block, states // 2, inner), lambda i: (seq, blocks - 1 - i, 0, 0)
                ),
                rows_of(inner),
                fixed((8, inner), 1),
                fixed((8, LANES), 1),
                fixed((LANES, inner), 1),
                fixed((2 * LANES, inner), 1),
                fixed((8, inner), 1),
                before_spec,
                fixed(shapes[3].shape, 1),
                fixed(shapes[4].shape, 1),
                any_spec,
                any_spec,
                any_spec,
            ],
            out_specs=[
                rows_of(inner),
                rows_of(states),
                rows_of(LANES),
                fixed(shapes[3].shape, 1),
                fixed(shapes[4].shape, 1),
            ],
            out_shape=shapes,
            scratch_shapes=[
                pltpu.VMEM((states // 2, inner), F32),
                pltpu.VMEM((CHUNK + 8, inner), F32),
                pltpu.VMEM((CHUNK + 16, inner), F32),
            ],
            input_output_aliases=aliases,
            compiler_params=params(1),
            cost_estimate=cost(25 * 10**9, length * inner * 16, length * heads * CHUNK),
            name="back",
        )(
            conv_x,
            conv_bc,
            step,
            cum,
            upstream,
            mixed_y,
            old_states,
            conv_in,
            taps[:, :inner],
            head_rows,
            spread1,
            spread2,
            skip_row,
            conv_in,
            *sums,
            *in_place,
        )

    arrived = lax.ppermute(out_other, "tensor", [(i, i ^ 1) for i in range(tensor)])
    grad_y, out_own, arrived = tie(grad_y, out_own, arrived)
    out_kept, out_leaving = zip(
        *(core_sums(out_own[:, seq], arrived[:, seq]) for seq in range(seqs))
    )
    grad_y, *flat_leaving = tie(grad_y, *sum(out_leaving, []))
    each = columns - 1
    out_leaving = [flat_leaving[i * each : (i + 1) * each] for i in range(seqs)]
    made = back(0, grad_y, None)
    made = back(1, grad_y, made)
    arrivals = [column_sends(sent) for sent in out_leaving]
    grad_in, grad_bc_part, grad_delta, tap_fold, head_fold = back(2, grad_y, made)
    grad_in, *flat_arrivals = tie(grad_in, *sum(arrivals, []))
    arrivals = [flat_arrivals[i * each : (i + 1) * each] for i in range(seqs)]

    bc_chip = chip_total(grad_bc_part)
    in_grad = weight_grad(normed, grad_in).astype(BF)

    in_parts = lax.all_to_all(in_grad, "dp", split_axis=0, concat_axis=0, tiled=True)
    grad_delta, in_grad, bc_chip = tie(grad_delta, in_grad, bc_chip)
    bc_moved = column_total_sends(bc_chip)
    normed_own, normed_other = pl.pallas_call(
        join_kernel,
        grid=(seqs, wide_blocks),
        in_specs=[
            scalar_spec,
            by_rows(inner),
            by_rows(inner),
            by_rows(LANES),
            pl.BlockSpec((model, inner), lambda s, t: (0, 0)),
            pl.BlockSpec((model, inner), lambda s, t: (0, 0)),
            pl.BlockSpec((model, LANES), lambda s, t: (0, (inner + states) // LANES)),
        ],
        out_specs=[partial_spec, partial_spec],
        out_shape=[seen((columns, seqs, length, share), BF)] * 2,
        compiler_params=params(2),
        cost_estimate=cost(33 * 10**9, tokens_here * (2 * model + 4 * inner)),
        name="join",
    )(
        starts,
        grad_gate,
        grad_in,
        grad_delta,
        second_weight,
        first_weight,
        first_weight,
    )
    normed_other, bc_moved = tie(normed_other, bc_moved)
    normed_arrived = lax.ppermute(normed_other, "tensor", [(i, i ^ 1) for i in range(tensor)])
    normed_kept, normed_leaving = core_sums(normed_own, normed_arrived)
    bc_total = finish_total(bc_chip, bc_moved)
    bc_total, in_parts, *normed_leaving = tie(bc_total, in_parts, *normed_leaving)
    normed_moved = column_sends(normed_leaving)
    out_sums = []
    for kept, moved in zip(out_kept, arrivals):
        for part in moved:
            kept = kept + part.astype(F32)
        out_sums.append(kept)
    result = (inputs_share + jnp.stack(out_sums)).astype(BF)

    grad_small, bc_tap_fold = pl.pallas_call(
        functools.partial(bc_kernel, kwidth),
        grid=(seqs,),
        in_specs=[per_seq(states), per_seq(states), fixed((8, states), 1), per_seq(LANES)],
        out_specs=[per_seq(states + LANES), fixed((8 * kwidth + 8, states), 1)],
        out_shape=[
            seen((seqs, length, states + LANES), BF),
            seen((8 * kwidth + 8, states)),
        ],
        scratch_shapes=[
            pltpu.VMEM((length + 8, states), F32),
            pltpu.VMEM((length + 8, states), F32),
        ],
        compiler_params=params(1),
        cost_estimate=cost(8 * 10**9, tokens_here * states * 12),
        name="bc_back",
    )(bc_total, bc_pre, taps[:, inner:], grad_delta)
    small_grad = weight_grad(normed, grad_small).astype(BF)
    small_parts = lax.all_to_all(small_grad, "dp", split_axis=0, concat_axis=0, tiled=True)
    early_wide = early_share.astype(F32)
    gate_share = early_wide[:, :inner]
    out_share = early_wide[:, inner:]
    in_share = sum_parts(in_parts)
    small_share = sum_parts(small_parts)
    bc_share = small_share[:, :states]
    dt_share = small_share[:, states : states + heads]
    gate_m = momentum_rate * zx_moment[:, 0, :] + gate_share
    out_m = momentum_rate * out_moment.T + out_share
    in_m = momentum_rate * zx_moment[:, 1, :] + in_share
    bc_m = momentum_rate * bc_moment + bc_share
    dt_m = momentum_rate * dt_moment + dt_share
    early = jnp.concatenate(
        [gate_share + momentum_rate * gate_m, out_share + momentum_rate * out_m], axis=1
    )
    late = jnp.concatenate(
        [in_share + momentum_rate * in_m, bc_share + momentum_rate * bc_m], axis=1
    )
    dt_input = dt_share + momentum_rate * dt_m
    squares = jnp.sum(dt_input * dt_input, axis=0)
    units, slots = gram_units(early, late, squares)
    factors = newton(units, slots)
    bc_rows = lax.dynamic_slice(first_weight, (share_start, inner), (share, states))
    normed_share = normed_kept
    for moved in normed_moved:
        normed_share = normed_share + moved.astype(F32)
    normed_share = normed_share + jnp.einsum(
        "btk,fk->btf", grad_small[:, :, :states], bc_rows, preferred_element_type=F32
    )

    gain_share = lax.dynamic_slice_in_dim(norm_gain, share_start, share, 0)
    weighted = normed_share * gain_share
    gain_grad_share = jnp.sum(normed_share * inputs_share * inv_rms, axis=(0, 1))
    gain_padded = lax.dynamic_update_slice_in_dim(
        jnp.zeros((model,), F32), gain_grad_share, share_start, 0
    )
    inner_rows = jnp.sum(weighted * inputs_share, axis=-1)
    final_sums = tensor_sum(jnp.concatenate([inner_rows.reshape(-1), gain_padded]))
    final_sums, factors = tie(final_sums, factors)
    inner_sum = final_sums[: seqs * length].reshape(seqs, length)
    gain_part = final_sums[seqs * length :]
    upstream_share = lax.dynamic_slice_in_dim(cotangent, share_start, share, 2).astype(F32)
    input_grad = (
        upstream_share
        + inv_rms * weighted
        - inputs_share * inv_rms**3 * (inner_sum / model)[..., None]
    )

    tap_sums = tap_fold.reshape(kwidth + 2, 8, inner).sum(axis=1)
    head_sums = head_fold.reshape(2, 8, LANES).sum(axis=1)[:, :heads]
    skip_grad = tap_sums[kwidth + 1].reshape(heads, head_width).sum(axis=1)
    pieces = [
        tap_sums[: kwidth + 1].reshape(-1),
        gain_fold.sum(axis=0),
        head_sums.reshape(-1),
        skip_grad,
        bc_tap_fold.reshape(kwidth + 1, 8, states).sum(axis=1).reshape(-1),
        gain_part,
    ]
    flat = dp_sum(jnp.concatenate(pieces))
    xpar_count = (kwidth + 2) * inner
    xpar_g = flat[:xpar_count].reshape(kwidth + 2, inner)
    head_g = flat[xpar_count : xpar_count + 3 * heads].reshape(3, heads)
    bcpar_g = flat[xpar_count + 3 * heads : -model].reshape(kwidth + 1, states)
    gain_g = flat[-model:]

    ortho, dt_scale = updates(early, late, factors, slots, heads)
    early_ortho = ortho[:, : 2 * inner]
    late_ortho = ortho[:, 2 * inner :]
    dt_ortho = dt_input * dt_scale
    shrink = 1.0 - matrix_rate * weight_decay
    zx_m = jnp.stack([gate_m, in_m], axis=1)
    zx_new = w_zx * shrink - matrix_rate * jnp.stack(
        [early_ortho[:, :inner], late_ortho[:, :inner]], axis=1
    )
    bc_new = state_proj_weight * shrink - matrix_rate * late_ortho[:, inner:]
    dt_new = step_weight * shrink - matrix_rate * dt_ortho
    out_new = exit_coefficient_matrix * shrink - matrix_rate * early_ortho[:, inner:].T
    gain_m = momentum_rate * gain_moment + gain_g
    xpar_m = momentum_rate * xpar_moment + xpar_g
    bcpar_m = momentum_rate * bcpar_moment + bcpar_g
    head_m = momentum_rate * head_moment + head_g
    gain_new = norm_gain - small_rate * (gain_g + momentum_rate * gain_m)
    xpar_new = x_params - small_rate * (xpar_g + momentum_rate * xpar_m)
    bcpar_new = bc_params - small_rate * (bcpar_g + momentum_rate * bcpar_m)
    head_new = head_params - small_rate * (head_g + momentum_rate * head_m)
    return (
        result,
        input_grad,
        zx_m,
        zx_new,
        bc_m,
        bc_new,
        dt_m,
        dt_new,
        out_m.T,
        out_new,
        gain_m,
        gain_new,
        xpar_m,
        xpar_new,
        bcpar_m,
        bcpar_new,
        head_m,
        head_new,
    )


def solution(mesh):
    return jax.shard_map(
        local,
        mesh=mesh,
        in_specs=(
            P("dp", None, None),
            P("dp", None, None),
            P(),
            P("dp", None, "tensor"),
            P("dp", None),
            P("dp", "tensor"),
            P("tensor", "dp"),
            P(None, "tensor"),
            P(),
            P(None, "tensor"),
            P("dp", None, "tensor"),
            P("dp", None),
            P("dp", "tensor"),
            P("tensor", "dp"),
            P(),
            P(None, "tensor"),
            P(),
            P(None, "tensor"),
        ),
        out_specs=(
            P("dp", None, "tensor"),
            P("dp", None, "tensor"),
            P("dp", None, "tensor"),
            P("dp", None, "tensor"),
            P("dp", None),
            P("dp", None),
            P("dp", "tensor"),
            P("dp", "tensor"),
            P("tensor", "dp"),
            P("tensor", "dp"),
            P(),
            P(),
            P(None, "tensor"),
            P(None, "tensor"),
            P(),
            P(),
            P(None, "tensor"),
            P(None, "tensor"),
        ),
        check_vma=False,
    )
```
